256 devices in a mesh: blk: 16 (over y, z_lo, core), rep: 16 (over x, z_hi).
Axes of the slice: x: 4, y: 4, z: 8 (z_hi: 4, z_lo: 2; z = z_hi * 2 + z_lo), core: 2. Of those that a mesh axis runs over, the one named last changes fastest.
Arguments:
- root_rows: float32 [256, 16384], P(None, 'blk'), may hold values from -520 to 520
- gradient: bfloat16 [2048, 16384], P('rep', 'blk'), may hold values from -6 to 6
Outputs:
- eigen_values: float32 [16384], P('blk')
- projected_energy: float32 [2048, 16384], P('rep', 'blk')
The draws below stay inside these ranges and needn't reach their ends.
All inputs are finite; a program needn't handle non-finite values.
Results may differ from the reference program's by a relative error of at most 0.0003.
Values sent between devices are 32-bit elements; how exact they have to be, the bound alone decides.
No kernel may reach another device: no remote copies, remote signals or barrier semaphores. Data moves between devices by JAX's collectives and lax.ppermute only.
A program may use at most 64 MiB of HBM per device.

```python
import math
import jax
import jax.numpy as jnp

ORDER = 16384
BLOCK = 512
ROOT_ROWS = 256
GRAD_ROWS = 2048
SWEEPS = 4
ROUNDS = 4


def draw_root_rows(key, part):
    key = jax.random.fold_in(key, 7)
    key_list = jax.random.split(key, 5)
    positions = jnp.arange(ROOT_ROWS, dtype=jnp.float32)[:, None] / ROOT_ROWS
    row_scale = jnp.exp(positions * math.log(3.0) + jax.random.uniform(key_list[0], (ROOT_ROWS, 1), jnp.float32, 0.0, math.log(3.4)))
    column_scale = jnp.exp(jax.random.uniform(key_list[1], (1, ORDER), jnp.float32, math.log(0.3), math.log(3.0)))
    base_part = jnp.clip(jax.random.normal(key_list[2], (ROOT_ROWS, ORDER), jnp.float32), -6.0, 6.0)
    common_weight = 0.8
    shared = jnp.clip(jax.random.normal(key_list[3], (ROOT_ROWS, 1), jnp.float32), -3.0, 3.0)
    loading = jnp.clip(jax.random.normal(key_list[4], (1, ORDER), jnp.float32), -3.0, 3.0)
    return row_scale * column_scale * (base_part + common_weight * shared * loading)


def shard_levels(rng, extent, pieces, least, top_value):
    factor_of = 1.0
    for axis_at, blocks in pieces:
        draws = jax.random.uniform(jax.random.fold_in(jax.random.fold_in(rng, 6), axis_at), (blocks,), jnp.float32, least / len(pieces), top_value / len(pieces))
        factor_of = factor_of * jnp.repeat(jnp.exp(draws), extent[axis_at] // blocks).reshape((-1,) + (1,) * (len(extent) - 1 - axis_at))
    return factor_of


def noise(rng, extent, deviation, limit, pieces=(), kind=jnp.bfloat16):
    entries = deviation * jax.random.normal(rng, extent, jnp.float32)
    if pieces:
        entries = entries * shard_levels(rng, extent, pieces, -0.22, 0.18)
    return jnp.clip(entries, -limit, limit).astype(kind)


def setup_inputs(seed: int = 0) -> dict:
    arg_keys = jax.random.split(jax.random.key(seed), 3)
    return {
        "root_rows": draw_root_rows(jax.random.fold_in(arg_keys[2], 71), 0),
        "gradient": noise(arg_keys[1], (GRAD_ROWS, ORDER), 1.0, 6.0, ((0, 16), (1, 16))),
    }


def rotate_pair(top_part, bottom_part, cosine, sine_part):
    return cosine * top_part + sine_part * bottom_part, cosine * bottom_part - sine_part * top_part


def reference(root_rows, gradient):
    slots = ORDER // (2 * BLOCK)
    shaped = root_rows.reshape(ROOT_ROWS, slots, 2, BLOCK)
    top_root = shaped[:, :, 0]
    bottom_root = shaped[:, :, 1]
    grad_shaped = gradient.astype(jnp.float32).reshape(GRAD_ROWS, slots, 2, BLOCK)
    top_grad = grad_shaped[:, :, 0]
    bottom_grad = grad_shaped[:, :, 1]
    for round_index in range(ROUNDS):
        for sweep_index in range(SWEEPS):
            top_square = jnp.sum(top_root * top_root, axis=0)
            bottom_square = jnp.sum(bottom_root * bottom_root, axis=0)
            cross_sum = jnp.sum(top_root * bottom_root, axis=0)
            angle_half = 0.5 * jnp.arctan2(2.0 * cross_sum, top_square - bottom_square)
            cosine = jnp.cos(angle_half)
            sine_part = jnp.sin(angle_half)
            top_root, bottom_root = rotate_pair(top_root, bottom_root, cosine, sine_part)
            top_grad, bottom_grad = rotate_pair(top_grad, bottom_grad, cosine, sine_part)
            bottom_root = jnp.roll(bottom_root, -1, axis=2)
            bottom_grad = jnp.roll(bottom_grad, -1, axis=2)
        if round_index + 1 < ROUNDS:
            top_root = jnp.roll(top_root, 1, axis=1)
            top_grad = jnp.roll(top_grad, 1, axis=1)
            bottom_root = jnp.roll(bottom_root, -1, axis=1)
            bottom_grad = jnp.roll(bottom_grad, -1, axis=1)
    bottom_root = jnp.roll(bottom_root, ROUNDS * SWEEPS, axis=2)
    bottom_grad = jnp.roll(bottom_grad, ROUNDS * SWEEPS, axis=2)
    column_sums = jnp.stack([jnp.sum(top_root * top_root, axis=0), jnp.sum(bottom_root * bottom_root, axis=0)], axis=1)
    eigen_values = column_sums.reshape(ORDER) * (1.0 / ROOT_ROWS)
    projected = jnp.stack([top_grad * top_grad, bottom_grad * bottom_grad], axis=2).reshape(GRAD_ROWS, ORDER)
    return eigen_values, projected
```

```python
import functools
import jax
import jax.numpy as jnp
from jax import lax
from jax.experimental import pallas as pl
from jax.experimental.pallas import tpu as pltpu
from jax.sharding import PartitionSpec as P

ROOT_ROWS = 256
SWEEPS = 4
WIDTH = 512
LANES = 128
HALO = 16
GROUPS = LANES // HALO
HALO_ROWS = ROOT_ROWS // GROUPS
CHUNK_ROWS = ROOT_ROWS + HALO_ROWS
PARTS = WIDTH // LANES
ROUND_PAIRS = (((0, 0), (1, 1), (2, 2)), ((0, 1), (1, 2)), ((0, 2),))
STEPS = SWEEPS * sum(len(pairs) for pairs in ROUND_PAIRS)
EIGEN_ROW = 2 * STEPS
ANGLE_ROWS = 2 * STEPS + 8
MEGA = 1 << 20


def turn_of(tt, bb, tb):
    y = 2.0 * tb
    x = tt - bb
    ax = jnp.abs(x)
    ay = jnp.abs(y)
    top = jnp.maximum(ax, ay)
    none = top == 0.0
    scale = 1.0 / jnp.where(none, 1.0, top)
    xs = jnp.where(none, 1.0, ax * scale)
    ys = jnp.where(none, 0.0, ay * scale)
    inv = lax.rsqrt(xs * xs + ys * ys)
    big = jnp.sqrt(0.5 + 0.5 * (xs * inv))
    small = 0.5 * (ys * inv) / big
    forward = x >= 0.0
    cosine = jnp.where(forward, big, small)
    size = jnp.where(forward, small, big)
    return cosine, jnp.where(y < 0.0, -size, size)


def total8(acc):
    return jnp.sum(acc, axis=0, keepdims=True)


def first_kernel(root_ref, top_out, both_out, bottom_out, turn_out, top, bottom):
    tile = 8
    count = ROOT_ROWS // tile
    zero = jnp.zeros((tile, WIDTH), jnp.float32)

    def measure(i, acc):
        rows = pl.ds(pl.multiple_of(i * tile, tile), tile)
        t = root_ref[rows, pl.ds(0, WIDTH)]
        b = root_ref[rows, pl.ds(WIDTH, WIDTH)]
        top[rows, :] = t
        bottom[rows, :] = b
        return acc[0] + t * t, acc[1] + b * b, acc[2] + t * b

    sums = lax.fori_loop(0, count, measure, (zero, zero, zero), unroll=4)
    for step in range(SWEEPS):
        cosine, sine = turn_of(*(total8(a) for a in sums))
        turn_out[pl.ds(step, 1), :] = cosine
        turn_out[pl.ds(SWEEPS + step, 1), :] = sine
        cb = jnp.broadcast_to(cosine, (tile, WIDTH))
        sb = jnp.broadcast_to(sine, (tile, WIDTH))

        def rotate(i, acc, cb=cb, sb=sb):
            rows = pl.ds(pl.multiple_of(i * tile, tile), tile)
            t = top[rows, :]
            b = bottom[rows, :]
            t, b = cb * t + sb * b, cb * b - sb * t
            b = pltpu.roll(b, WIDTH - 1, 1)
            top[rows, :] = t
            bottom[rows, :] = b
            return acc[0] + t * t, acc[1] + b * b, acc[2] + t * b

        sums = lax.fori_loop(0, count, rotate, (zero, zero, zero), unroll=4)

    part = lax.axis_index("rep") // PARTS
    here = pl.ds(pl.multiple_of(part * LANES, LANES), LANES)
    after = pl.ds(pl.multiple_of(lax.rem(part + 1, PARTS) * LANES, LANES), LANES)
    lane_group = lax.broadcasted_iota(jnp.int32, (8, LANES), 1) // HALO

    def folded(block, q):
        out = block[pl.ds(8 * q, 8), after]
        for g in range(1, GROUPS):
            piece = block[pl.ds(g * HALO_ROWS + 8 * q, 8), after]
            out = jnp.where(lane_group == g, pltpu.roll(piece, g * HALO, 1), out)
        return out

    t = top[:, here]
    b = bottom[:, here]
    top_out[pl.ds(0, ROOT_ROWS), :] = t
    both_out[pl.ds(0, ROOT_ROWS), :] = t
    bottom_out[pl.ds(0, ROOT_ROWS), :] = b
    both_out[pl.ds(CHUNK_ROWS, ROOT_ROWS), :] = b
    for q in range(HALO_ROWS // 8):
        t = folded(top, q)
        b = folded(bottom, q)
        top_out[pl.ds(ROOT_ROWS + 8 * q, 8), :] = t
        both_out[pl.ds(ROOT_ROWS + 8 * q, 8), :] = t
        bottom_out[pl.ds(ROOT_ROWS + 8 * q, 8), :] = b
        both_out[pl.ds(CHUNK_ROWS + ROOT_ROWS + 8 * q, 8), :] = b


def gradient_first_kernel(grad_ref, turn_ref, top_out, both_out, bottom_out):
    tile = 16
    count = grad_ref.shape[0] // tile

    def body(i, carry):
        rows = pl.ds(pl.multiple_of(i * tile, tile), tile)
        t = grad_ref[rows, pl.ds(0, WIDTH)].astype(jnp.float32)
        b = grad_ref[rows, pl.ds(WIDTH, WIDTH)].astype(jnp.float32)
        for step in range(SWEEPS):
            c = turn_ref[pl.ds(step, 1), :]
            s = turn_ref[pl.ds(SWEEPS + step, 1), :]
            t, b = c * t + s * b, c * b - s * t
            b = pltpu.roll(b, WIDTH - 1, 1)
        top_out[rows, :] = t
        both_out[rows, :] = t
        bottom_out[rows, :] = b
        both_out[pl.ds(pl.multiple_of(i * tile + grad_ref.shape[0], tile), tile), :] = b
        return carry

    lax.fori_loop(0, count, body, 0)


def cone_kernel(top0, pair1, pair2, bottom2, turn_out, blocks):
    lane = lax.broadcasted_iota(jnp.int32, (8, LANES), 1)
    last = lane == LANES - 1
    main_count = ROOT_ROWS // 8
    halo_count = HALO_ROWS // 8
    zero = jnp.zeros((8, LANES), jnp.float32)
    blocks[0] = top0[...]
    blocks[1] = pair1[pl.ds(0, CHUNK_ROWS), :]
    blocks[3] = pair1[pl.ds(CHUNK_ROWS, CHUNK_ROWS), :]
    blocks[2] = pair2[pl.ds(0, CHUNK_ROWS), :]
    blocks[4] = pair2[pl.ds(CHUNK_ROWS, CHUNK_ROWS), :]
    blocks[5] = bottom2[...]

    def halo_total(acc):
        row = total8(acc)
        for by in (HALO, 2 * HALO, 4 * HALO):
            row = row + pltpu.roll(row, by, 1)
        return row

    def sums_of(pairs):
        out = []
        for ti, bi in pairs:
            for first, count, fold in ((0, main_count, total8), (main_count, halo_count, halo_total)):
                acc = (zero, zero, zero)
                for v in range(count):
                    rows = pl.ds(8 * (first + v), 8)
                    t = blocks[ti, rows, :]
                    b = blocks[3 + bi, rows, :]
                    acc = acc[0] + t * t, acc[1] + b * b, acc[2] + t * b
                out.append(tuple(fold(a) for a in acc))
        return out

    def stacked(sums):
        pad = [jnp.zeros((1, LANES), jnp.float32)] * (8 - len(sums))
        return tuple(jnp.concatenate([s[j] for s in sums] + pad, axis=0) for j in range(3))

    base = 0
    for pairs in ROUND_PAIRS:
        n = len(pairs)

        def step_body(k, sums, pairs=pairs, n=n, base=base):
            cosine, sine = turn_of(*sums)
            out = []
            for p, (ti, bi) in enumerate(pairs):
                row = base + p * SWEEPS + k
                turn_out[0, pl.ds(row, 1), :] = cosine[2 * p : 2 * p + 1]
                turn_out[0, pl.ds(STEPS + row, 1), :] = sine[2 * p : 2 * p + 1]
                c = jnp.broadcast_to(cosine[2 * p + 1 : 2 * p + 2], (8, LANES))
                s = jnp.broadcast_to(sine[2 * p + 1 : 2 * p + 2], (8, LANES))
                hacc = (zero, zero, zero)
                turned = []
                for v in range(halo_count):
                    rows = pl.ds(8 * (main_count + v), 8)
                    t = blocks[ti, rows, :]
                    b = blocks[3 + bi, rows, :]
                    t, b = c * t + s * b, c * b - s * t
                    turned.append(b)
                    b = pltpu.roll(b, LANES - 1, 1)
                    blocks[ti, rows, :] = t
                    blocks[3 + bi, rows, :] = b
                    hacc = hacc[0] + t * t, hacc[1] + b * b, hacc[2] + t * b
                c = jnp.broadcast_to(cosine[2 * p : 2 * p + 1], (8, LANES))
                s = jnp.broadcast_to(sine[2 * p : 2 * p + 1], (8, LANES))
                acc = (zero, zero, zero)
                for v in range(main_count):
                    rows = pl.ds(8 * v, 8)
                    t = blocks[ti, rows, :]
                    b = blocks[3 + bi, rows, :]
                    t, b = c * t + s * b, c * b - s * t
                    g, q = divmod(8 * v, HALO_ROWS)
                    entering = pltpu.roll(turned[q // 8], LANES - 1 - g * HALO, 1)
                    b = jnp.where(last, entering, pltpu.roll(b, LANES - 1, 1))
                    blocks[ti, rows, :] = t
                    blocks[3 + bi, rows, :] = b
                    acc = acc[0] + t * t, acc[1] + b * b, acc[2] + t * b
                out.append(tuple(total8(a) for a in acc))
                out.append(tuple(halo_total(a) for a in hacc))
            return stacked(out)

        sums = lax.fori_loop(0, SWEEPS, step_body, stacked(sums_of(pairs)))
        base += n * SWEEPS
    turn_out[0, pl.ds(EIGEN_ROW, 1), :] = sums[0][0:1] * (1.0 / ROOT_ROWS)
    turn_out[0, pl.ds(EIGEN_ROW + 1, 1), :] = sums[1][0:1] * (1.0 / ROOT_ROWS)
    turn_out[0, pl.ds(EIGEN_ROW + 2, 6), :] = jnp.zeros((6, LANES), jnp.float32)
    for copy in range(1, PARTS):
        turn_out[copy] = turn_out[0]


def last_kernel(top0, pair1, pair2, bottom2, turns, eigen_out, projected_out, wide):
    tile = 8
    rows_all = top0.shape[0]
    for part in range(PARTS):
        wide[:, pl.ds(part * LANES, LANES)] = turns[part]

    def body(i, carry):
        rows = pl.ds(pl.multiple_of(i * tile, tile), tile)
        low = pl.ds(pl.multiple_of(i * tile + rows_all, tile), tile)
        tops = [top0[rows, :], pair1[rows, :], pair2[rows, :]]
        bottoms = [pair1[low, :], pair2[low, :], bottom2[rows, :]]
        base = 0
        for pairs in ROUND_PAIRS:
            for k in range(SWEEPS):
                for p, (ti, bi) in enumerate(pairs):
                    row = base + p * SWEEPS + k
                    c = wide[pl.ds(row, 1), :]
                    s = wide[pl.ds(STEPS + row, 1), :]
                    t, b = tops[ti], bottoms[bi]
                    tops[ti], b = c * t + s * b, c * b - s * t
                    bottoms[bi] = pltpu.roll(b, WIDTH - 1, 1)
            base += len(pairs) * SWEEPS
        t = tops[0]
        b = pltpu.roll(bottoms[2], 4 * SWEEPS, 1)
        projected_out[rows, pl.ds(0, WIDTH)] = t * t
        projected_out[rows, pl.ds(WIDTH, WIDTH)] = b * b
        return carry

    lax.fori_loop(0, rows_all // tile, body, 0)
    eigen_out[pl.ds(0, 1), :] = wide[pl.ds(EIGEN_ROW, 1), :]
    eigen_out[pl.ds(1, 1), :] = pltpu.roll(wide[pl.ds(EIGEN_ROW + 1, 1), :], 4 * SWEEPS, 1)


def call(kernel, outs, scratch, args, flops):
    f32 = jnp.float32
    vmem = pl.BlockSpec(memory_space=pltpu.VMEM)
    shapes = tuple(jax.ShapeDtypeStruct(shape, f32) for shape in outs)
    moved = sum(a.size * a.dtype.itemsize for a in args) + sum(4 * s.size for s in shapes)
    return pl.pallas_call(
        kernel,
        out_shape=shapes,
        in_specs=[vmem] * len(args),
        out_specs=tuple(vmem for _ in shapes),
        scratch_shapes=[pltpu.VMEM(shape, f32) for shape in scratch],
        compiler_params=pltpu.CompilerParams(vmem_limit_bytes=24 * MEGA),
        cost_estimate=pl.CostEstimate(flops=flops, bytes_accessed=moved, transcendentals=0),
    )(*args)


def from_slot(shard, offset):
    length = lax.axis_size("blk")
    return lax.ppermute(shard, "blk", [((i + offset) % length, i) for i in range(length)])


def body(root_rows, gradient):
    rows = gradient.shape[0]
    top_root, both_root, bottom_root, turn0 = call(
        first_kernel,
        [(CHUNK_ROWS, LANES), (2 * CHUNK_ROWS, LANES), (CHUNK_ROWS, LANES), (2 * SWEEPS, WIDTH)],
        [(ROOT_ROWS, WIDTH), (ROOT_ROWS, WIDTH)],
        [root_rows],
        16 * ROOT_ROWS * WIDTH * SWEEPS,
    )
    root3 = from_slot(bottom_root, 3)
    root0 = from_slot(top_root, -3)
    root1 = from_slot(both_root, -1)
    root2 = from_slot(both_root, 1)
    top_grad, both_grad, bottom_grad = call(
        gradient_first_kernel,
        [(rows, WIDTH), (2 * rows, WIDTH), (rows, WIDTH)],
        [],
        [gradient, turn0],
        8 * rows * WIDTH * SWEEPS,
    )
    grad1 = from_slot(both_grad, -1)
    grad2 = from_slot(both_grad, 1)
    grad0 = from_slot(top_grad, -3)
    grad3 = from_slot(bottom_grad, 3)
    (turns,) = call(
        cone_kernel,
        [(PARTS, ANGLE_ROWS, LANES)],
        [(6, CHUNK_ROWS, LANES)],
        [root0, root1, root2, root3],
        16 * CHUNK_ROWS * LANES * STEPS,
    )
    reps = lax.axis_size("rep")
    near = reps // PARTS
    groups = [[x * near + z for x in range(PARTS)] for z in range(near)]
    turns = lax.all_to_all(turns, "rep", 0, 0, axis_index_groups=groups)
    eigen, projected = call(
        last_kernel,
        [(2, WIDTH), (rows, 2 * WIDTH)],
        [(ANGLE_ROWS, WIDTH)],
        [grad0, grad1, grad2, grad3, turns],
        8 * rows * WIDTH * STEPS,
    )
    return eigen.reshape(2 * WIDTH), projected


def solution(mesh):
    return jax.shard_map(
        body,
        mesh=mesh,
        in_specs=(P(None, "blk"), P("rep", "blk")),
        out_specs=(P("blk"), P("rep", "blk")),
        check_vma=False,
    )
```

```python
import functools
import jax
import jax.numpy as jnp
from jax import lax
from jax.experimental import pallas as pl
from jax.experimental.pallas import tpu as pltpu
from jax.sharding import PartitionSpec as P

ROOT_ROWS = 256
SWEEPS = 4
WIDTH = 512
LANES = 128
HALO = 16
GROUPS = LANES // HALO
HALO_ROWS = ROOT_ROWS // GROUPS
CHUNK_ROWS = ROOT_ROWS + HALO_ROWS
PARTS = WIDTH // LANES
ROUND_PAIRS = (((0, 0), (1, 1), (2, 2)), ((0, 1), (1, 2)), ((0, 2),))
STEPS = SWEEPS * sum(len(pairs) for pairs in ROUND_PAIRS)
EIGEN_ROW = 2 * STEPS
ANGLE_ROWS = 2 * STEPS + 8
MEGA = 1 << 20


def turn_of(tt, bb, tb):
    y = 2.0 * tb
    x = tt - bb
    ax = jnp.abs(x)
    ay = jnp.abs(y)
    top = jnp.maximum(ax, ay)
    none = top == 0.0
    scale = 1.0 / jnp.where(none, 1.0, top)
    xs = jnp.where(none, 1.0, ax * scale)
    ys = jnp.where(none, 0.0, ay * scale)
    inv = lax.rsqrt(xs * xs + ys * ys)
    big = jnp.sqrt(0.5 + 0.5 * (xs * inv))
    small = 0.5 * (ys * inv) / big
    forward = x >= 0.0
    cosine = jnp.where(forward, big, small)
    size = jnp.where(forward, small, big)
    return cosine, jnp.where(y < 0.0, -size, size)


def total8(acc):
    return jnp.sum(acc, axis=0, keepdims=True)


def turned_sums(source, target, cosine, sine, count):
    acc = None
    if cosine is not None:
        cosine = jnp.broadcast_to(cosine, (8, WIDTH))
        sine = jnp.broadcast_to(sine, (8, WIDTH))
    for i in range(count):
        t, b = source(i)
        if cosine is not None:
            t, b = cosine * t + sine * b, cosine * b - sine * t
            b = pltpu.roll(b, WIDTH - 1, 1)
            target(i, t, b)
        new = t * t, b * b, t * b
        acc = new if acc is None else tuple(x + y for x, y in zip(acc, new))
    return tuple(total8(x) for x in acc)


def first_kernel(root_ref, top_out, both_out, bottom_out, turn_out, top, bottom):
    count = ROOT_ROWS // 8

    def given(i):
        rows = pl.ds(8 * i, 8)
        return root_ref[rows, pl.ds(0, WIDTH)], root_ref[rows, pl.ds(WIDTH, WIDTH)]

    def kept(i):
        rows = pl.ds(8 * i, 8)
        return top[rows, :], bottom[rows, :]

    def keep(i, t, b):
        rows = pl.ds(8 * i, 8)
        top[rows, :] = t
        bottom[rows, :] = b

    def turn(step, sums):
        cosine, sine = turn_of(*sums)
        turn_out[pl.ds(step, 1), :] = cosine
        turn_out[pl.ds(SWEEPS + step, 1), :] = sine
        return cosine, sine

    sums = turned_sums(given, None, None, None, count)
    sums = turned_sums(given, keep, *turn(0, sums), count)
    lax.fori_loop(
        1, SWEEPS, lambda step, sums: turned_sums(kept, keep, *turn(step, sums), count), sums
    )

    part = lax.axis_index("rep") // PARTS
    here = pl.ds(pl.multiple_of(part * LANES, LANES), LANES)
    after = pl.ds(pl.multiple_of(lax.rem(part + 1, PARTS) * LANES, LANES), LANES)
    lane_group = lax.broadcasted_iota(jnp.int32, (8, LANES), 1) // HALO

    def folded(block, q):
        out = block[pl.ds(8 * q, 8), after]
        for g in range(1, GROUPS):
            piece = block[pl.ds(g * HALO_ROWS + 8 * q, 8), after]
            out = jnp.where(lane_group == g, pltpu.roll(piece, g * HALO, 1), out)
        return out

    t = top[:, here]
    b = bottom[:, here]
    top_out[pl.ds(0, ROOT_ROWS), :] = t
    both_out[pl.ds(0, ROOT_ROWS), :] = t
    bottom_out[pl.ds(0, ROOT_ROWS), :] = b
    both_out[pl.ds(CHUNK_ROWS, ROOT_ROWS), :] = b
    for q in range(HALO_ROWS // 8):
        t = folded(top, q)
        b = folded(bottom, q)
        top_out[pl.ds(ROOT_ROWS + 8 * q, 8), :] = t
        both_out[pl.ds(ROOT_ROWS + 8 * q, 8), :] = t
        bottom_out[pl.ds(ROOT_ROWS + 8 * q, 8), :] = b
        both_out[pl.ds(CHUNK_ROWS + ROOT_ROWS + 8 * q, 8), :] = b


def gradient_first_kernel(grad_ref, turn_ref, top_out, both_out, bottom_out):
    rows_all = grad_ref.shape[0]
    tiles = [pl.ds(8 * i, 8) for i in range(rows_all // 8)]
    for step in range(SWEEPS):
        c = jnp.broadcast_to(turn_ref[pl.ds(step, 1), :], (8, WIDTH))
        s = jnp.broadcast_to(turn_ref[pl.ds(SWEEPS + step, 1), :], (8, WIDTH))
        for i, rows in enumerate(tiles):
            low = pl.ds(rows_all + 8 * i, 8)
            if step == 0:
                if i % 2 == 0:
                    pair = grad_ref[pl.ds(8 * i, 16), :].astype(jnp.float32)
                half = pair[:8] if i % 2 == 0 else pair[8:]
                t, b = half[:, :WIDTH], half[:, WIDTH:]
            else:
                t, b = top_out[rows, :], bottom_out[rows, :]
            t, b = c * t + s * b, c * b - s * t
            b = pltpu.roll(b, WIDTH - 1, 1)
            top_out[rows, :] = t
            bottom_out[rows, :] = b
            if step == SWEEPS - 1:
                both_out[rows, :] = t
                both_out[low, :] = b


def cone_kernel(top0, pair1, pair2, bottom2, turn_out, blocks):
    count = ROOT_ROWS // 8
    per_group = HALO_ROWS // 8
    lane = lax.broadcasted_iota(jnp.int32, (8, LANES), 1)
    last = lane == LANES - 1
    lane_group = lane // HALO
    homes = ((top0, 0), (pair1, 0), (pair2, 0), (pair1, CHUNK_ROWS), (pair2, CHUNK_ROWS), (bottom2, 0))

    def unfolded(places, i):
        g, q = divmod(i, per_group)
        out = None
        for p, (ref, first) in enumerate(places):
            piece = ref[pl.ds(first + ROOT_ROWS + 8 * q, 8), :]
            piece = pltpu.roll(piece, (p - g) * HALO % LANES, 1)
            out = piece if out is None else jnp.where(lane_group == p, piece, out)
        return out

    def given(index, i):
        rows = pl.ds(8 * i, 8)
        if index < 6:
            ref, first = homes[index]
            return ref[pl.ds(first + 8 * i, 8), :]
        return blocks[index, rows, :]

    for i in range(count):
        rows = pl.ds(8 * i, 8)
        blocks[6, rows, :] = unfolded(homes[:3], i)
        blocks[7, rows, :] = unfolded(homes[3:], i)

    def all_of(pairs):
        return [(ti, 3 + bi) for ti, bi in pairs] + [(6, 7)]

    def sums_of(pairs, fetch):
        acc = [None] * (len(pairs) + 1)
        for i in range(count):
            for p, (ti, bi) in enumerate(all_of(pairs)):
                t, b = fetch(ti, i), fetch(bi, i)
                new = t * t, b * b, t * b
                acc[p] = new if acc[p] is None else tuple(x + y for x, y in zip(acc[p], new))
        return stacked(acc)

    def stacked(acc):
        pad = [jnp.zeros((1, LANES), jnp.float32)] * (4 - len(acc))
        return tuple(jnp.concatenate([total8(a[j]) for a in acc] + pad, axis=0) for j in range(3))

    def stored(index, i):
        return blocks[index, pl.ds(8 * i, 8), :]

    def step(k, sums, pairs, base, fetch):
        n = len(pairs)
        cosine, sine = turn_of(*sums)
        for p in range(n):
            row = base + p * SWEEPS + k
            turn_out[0, pl.ds(row, 1), :] = cosine[p : p + 1]
            turn_out[0, pl.ds(STEPS + row, 1), :] = sine[p : p + 1]
        cs = [jnp.broadcast_to(cosine[p : p + 1], (8, LANES)) for p in range(n + 1)]
        sn = [jnp.broadcast_to(sine[p : p + 1], (8, LANES)) for p in range(n + 1)]
        acc = [None] * (n + 1)
        for i in range(count):
            rows = pl.ds(8 * i, 8)
            t, b = stored(6, i), stored(7, i)
            t, halo = cs[n] * t + sn[n] * b, cs[n] * b - sn[n] * t
            b = pltpu.roll(halo, LANES - 1, 1)
            turned = [(t, b)]
            for p, (ti, bi) in enumerate(all_of(pairs)[:n]):
                t, b = fetch(ti, i), fetch(bi, i)
                t, b = cs[p] * t + sn[p] * b, cs[p] * b - sn[p] * t
                entering = pltpu.roll(halo, LANES - 1 - p * HALO, 1)
                b = jnp.where(last, entering, pltpu.roll(b, LANES - 1, 1))
                turned.append((t, b))
            turned = turned[1:] + turned[:1]
            for p, (ti, bi) in enumerate(all_of(pairs)):
                t, b = turned[p]
                blocks[ti, rows, :] = t
                blocks[bi, rows, :] = b
                new = t * t, b * b, t * b
                acc[p] = new if acc[p] is None else tuple(x + y for x, y in zip(acc[p], new))
        return stacked(acc)

    base = 0
    for number, pairs in enumerate(ROUND_PAIRS):
        fetch = given if number == 0 else stored
        if number > 0:
            for i in range(count):
                rows = pl.ds(8 * i, 8)
                blocks[7, rows, :] = pltpu.roll(blocks[7, rows, :], LANES - HALO, 1)
        sums = sums_of(pairs, fetch)
        first = 0
        if number == 0:
            sums = step(0, sums, pairs, base, fetch)
            first = 1
        sums = lax.fori_loop(
            first,
            SWEEPS,
            functools.partial(step, pairs=pairs, base=base, fetch=stored),
            sums,
        )
        base += len(pairs) * SWEEPS
    turn_out[0, pl.ds(EIGEN_ROW, 1), :] = sums[0][0:1] * (1.0 / ROOT_ROWS)
    turn_out[0, pl.ds(EIGEN_ROW + 1, 1), :] = sums[1][0:1] * (1.0 / ROOT_ROWS)
    turn_out[0, pl.ds(EIGEN_ROW + 2, 6), :] = jnp.zeros((6, LANES), jnp.float32)
    for copy in range(1, PARTS):
        turn_out[copy] = turn_out[0]


def last_kernel(top0, pair1, pair2, bottom2, turns, eigen_out, projected_out, wide, blocks):
    rows_all = top0.shape[0]
    count = rows_all // 8
    for part in range(PARTS):
        wide[:, pl.ds(part * LANES, LANES)] = turns[part]

    def given(index, i):
        rows, low = pl.ds(8 * i, 8), pl.ds(rows_all + 8 * i, 8)
        return (
            lambda: top0[rows, :],
            lambda: pair1[rows, :],
            lambda: pair2[rows, :],
            lambda: pair1[low, :],
            lambda: pair2[low, :],
            lambda: bottom2[rows, :],
        )[index]()

    def one_step(base, pairs, k, fresh):
        for p, (ti, bi) in enumerate(pairs):
            row = base + p * SWEEPS + k
            c = jnp.broadcast_to(wide[pl.ds(row, 1), :], (8, WIDTH))
            s = jnp.broadcast_to(wide[pl.ds(STEPS + row, 1), :], (8, WIDTH))
            for i in range(count):
                rows = pl.ds(8 * i, 8)
                if fresh:
                    t, b = given(ti, i), given(3 + bi, i)
                else:
                    t, b = blocks[ti, rows, :], blocks[3 + bi, rows, :]
                t, b = c * t + s * b, c * b - s * t
                blocks[ti, rows, :] = t
                blocks[3 + bi, rows, :] = pltpu.roll(b, WIDTH - 1, 1)

    base = 0
    for number, pairs in enumerate(ROUND_PAIRS):
        first = 0
        if number == 0:
            one_step(base, pairs, 0, True)
            first = 1

        def body(k, carry, base=base, pairs=pairs):
            one_step(base, pairs, k, False)
            return carry

        lax.fori_loop(first, SWEEPS, body, 0)
        base += len(pairs) * SWEEPS
    for i in range(count):
        rows = pl.ds(8 * i, 8)
        t = blocks[0, rows, :]
        b = pltpu.roll(blocks[5, rows, :], 4 * SWEEPS, 1)
        projected_out[rows, pl.ds(0, WIDTH)] = t * t
        projected_out[rows, pl.ds(WIDTH, WIDTH)] = b * b
    eigen_out[pl.ds(0, 1), :] = wide[pl.ds(EIGEN_ROW, 1), :]
    eigen_out[pl.ds(1, 1), :] = pltpu.roll(wide[pl.ds(EIGEN_ROW + 1, 1), :], 4 * SWEEPS, 1)


def call(kernel, outs, scratch, args, flops):
    f32 = jnp.float32
    vmem = pl.BlockSpec(memory_space=pltpu.VMEM)
    shapes = tuple(jax.ShapeDtypeStruct(shape, f32) for shape in outs)
    moved = sum(a.size * a.dtype.itemsize for a in args) + sum(4 * s.size for s in shapes)
    return pl.pallas_call(
        kernel,
        out_shape=shapes,
        in_specs=[vmem] * len(args),
        out_specs=tuple(vmem for _ in shapes),
        scratch_shapes=[pltpu.VMEM(shape, f32) for shape in scratch],
        compiler_params=pltpu.CompilerParams(vmem_limit_bytes=24 * MEGA),
        cost_estimate=pl.CostEstimate(flops=flops, bytes_accessed=moved, transcendentals=0),
    )(*args)


def from_slot(shard, offset):
    length = lax.axis_size("blk")
    return lax.ppermute(shard, "blk", [((i + offset) % length, i) for i in range(length)])


def body(root_rows, gradient):
    rows = gradient.shape[0]
    top_root, both_root, bottom_root, turn0 = call(
        first_kernel,
        [(CHUNK_ROWS, LANES), (2 * CHUNK_ROWS, LANES), (CHUNK_ROWS, LANES), (2 * SWEEPS, WIDTH)],
        [(ROOT_ROWS, WIDTH), (ROOT_ROWS, WIDTH)],
        [root_rows],
        16 * ROOT_ROWS * WIDTH * SWEEPS,
    )
    root3 = from_slot(bottom_root, 3)
    root0 = from_slot(top_root, -3)
    root1 = from_slot(both_root, -1)
    root2 = from_slot(both_root, 1)
    turn0, root0 = lax.optimization_barrier((turn0, root0))
    top_grad, both_grad, bottom_grad = call(
        gradient_first_kernel,
        [(rows, WIDTH), (2 * rows, WIDTH), (rows, WIDTH)],
        [],
        [gradient, turn0],
        8 * rows * WIDTH * SWEEPS,
    )
    grad1 = from_slot(both_grad, -1)
    grad2 = from_slot(both_grad, 1)
    grad0 = from_slot(top_grad, -3)
    grad3 = from_slot(bottom_grad, 3)
    (turns,) = call(
        cone_kernel,
        [(PARTS, ANGLE_ROWS, LANES)],
        [(8, ROOT_ROWS, LANES)],
        [root0, root1, root2, root3],
        16 * CHUNK_ROWS * LANES * STEPS,
    )
    reps = lax.axis_size("rep")
    near = reps // PARTS
    groups = [[x * near + z for x in range(PARTS)] for z in range(near)]
    turns = lax.all_to_all(turns, "rep", 0, 0, axis_index_groups=groups)
    eigen, projected = call(
        last_kernel,
        [(2, WIDTH), (rows, 2 * WIDTH)],
        [(ANGLE_ROWS, WIDTH), (6, rows, WIDTH)],
        [grad0, grad1, grad2, grad3, turns],
        8 * rows * WIDTH * STEPS,
    )
    return eigen.reshape(2 * WIDTH), projected


def solution(mesh):
    return jax.shard_map(
        body,
        mesh=mesh,
        in_specs=(P(None, "blk"), P("rep", "blk")),
        out_specs=(P("blk"), P("rep", "blk")),
        check_vma=False,
    )
```

```python
import functools
import jax
import jax.numpy as jnp
from jax import lax
from jax.experimental import pallas as pl
from jax.experimental.pallas import tpu as pltpu
from jax.sharding import PartitionSpec as P

ROOT_ROWS = 256
SWEEPS = 4
WIDTH = 512
LANES = 128
HALO = 16
GROUPS = LANES // HALO
HALO_ROWS = ROOT_ROWS // GROUPS
CHUNK_ROWS = ROOT_ROWS + HALO_ROWS
PARTS = WIDTH // LANES
ROUND_PAIRS = (((0, 0), (1, 1), (2, 2)), ((0, 1), (1, 2)), ((0, 2),))
STEPS = SWEEPS * sum(len(pairs) for pairs in ROUND_PAIRS)
EIGEN_ROW = 2 * STEPS
ANGLE_ROWS = 2 * STEPS + 8
MEGA = 1 << 20


def turn_of(tt, bb, tb):
    y = 2.0 * tb
    x = tt - bb
    ax = jnp.abs(x)
    ay = jnp.abs(y)
    top = jnp.maximum(ax, ay)
    none = top == 0.0
    scale = 1.0 / jnp.where(none, 1.0, top)
    xs = jnp.where(none, 1.0, ax * scale)
    ys = jnp.where(none, 0.0, ay * scale)
    squares = xs * xs + ys * ys
    inv = lax.rsqrt(squares)
    big = jnp.sqrt(0.5 + 0.5 * (xs * inv))
    small = 0.5 * (ys * inv) / big
    forward = x >= 0.0
    cosine = jnp.where(forward, big, small)
    size = jnp.where(forward, small, big)
    larger = 0.5 * (tt + bb) + 0.5 * (top * (squares * inv))
    return cosine, jnp.where(y < 0.0, -size, size), larger


def total8(acc):
    return jnp.sum(acc, axis=0, keepdims=True)


def added(acc, *new):
    return list(new) if acc is None else [x + y for x, y in zip(acc, new)]


def wide8(row):
    return jnp.broadcast_to(row, (8, LANES))


def first_kernel(root_ref, top_out, both_out, bottom_out, turn_out, top, bottom, rolled):
    tiles = [pl.ds(8 * i, 8) for i in range(ROOT_ROWS // 8)]
    cols = [pl.ds(g * LANES, LANES) for g in range(PARTS)]
    low_cols = [pl.ds(WIDTH + g * LANES, LANES) for g in range(PARTS)]
    last = lax.broadcasted_iota(jnp.int32, (8, LANES), 1) == LANES - 1
    tt, bb, tb = ([None] * PARTS for _ in range(3))
    for g in range(PARTS):
        acc = None
        for rows in tiles:
            t, b = root_ref[rows, cols[g]], root_ref[rows, low_cols[g]]
            acc = added(acc, b * b, t * b, t * t)
        bb[g], tb[g], tt[g] = (total8(x) for x in acc)

    def rotate(step, g):
        cosine, sine, tt[g] = turn_of(tt[g], bb[g], tb[g])
        turn_out[pl.ds(step, 1), cols[g]] = cosine
        turn_out[pl.ds(SWEEPS + step, 1), cols[g]] = sine
        c, s = wide8(cosine), wide8(sine)
        for rows in tiles:
            if step == 0:
                t, b = root_ref[rows, cols[g]], root_ref[rows, low_cols[g]]
            else:
                t, b = top[rows, cols[g]], bottom[rows, cols[g]]
            top[rows, cols[g]] = c * t + s * b
            rolled[rows, cols[g]] = pltpu.roll(c * b - s * t, LANES - 1, 1)

    def shift(step, g):
        acc = None
        for rows in tiles:
            b = jnp.where(last, rolled[rows, cols[(g + 1) % PARTS]], rolled[rows, cols[g]])
            bottom[rows, cols[g]] = b
            if step + 1 < SWEEPS:
                acc = added(acc, b * b, top[rows, cols[g]] * b)
        if step + 1 < SWEEPS:
            bb[g], tb[g] = (total8(x) for x in acc)

    for step in range(SWEEPS):
        rotate(step, 0)
        for g in range(1, PARTS):
            rotate(step, g)
            shift(step, g - 1)
        shift(step, PARTS - 1)

    part = lax.axis_index("rep") // PARTS
    here = pl.ds(pl.multiple_of(part * LANES, LANES), LANES)
    after = pl.ds(pl.multiple_of(lax.rem(part + 1, PARTS) * LANES, LANES), LANES)
    lane_group = lax.broadcasted_iota(jnp.int32, (8, LANES), 1) // HALO

    def folded(block, q):
        out = block[pl.ds(8 * q, 8), after]
        for g in range(1, GROUPS):
            piece = block[pl.ds(g * HALO_ROWS + 8 * q, 8), after]
            out = jnp.where(lane_group == g, pltpu.roll(piece, g * HALO, 1), out)
        return out

    t = top[:, here]
    b = bottom[:, here]
    top_out[pl.ds(0, ROOT_ROWS), :] = t
    both_out[pl.ds(0, ROOT_ROWS), :] = t
    bottom_out[pl.ds(0, ROOT_ROWS), :] = b
    both_out[pl.ds(CHUNK_ROWS, ROOT_ROWS), :] = b
    for q in range(HALO_ROWS // 8):
        t = folded(top, q)
        b = folded(bottom, q)
        top_out[pl.ds(ROOT_ROWS + 8 * q, 8), :] = t
        both_out[pl.ds(ROOT_ROWS + 8 * q, 8), :] = t
        bottom_out[pl.ds(ROOT_ROWS + 8 * q, 8), :] = b
        both_out[pl.ds(CHUNK_ROWS + ROOT_ROWS + 8 * q, 8), :] = b


def gradient_first_kernel(grad_ref, turn_ref, top_out, both_out, bottom_out):
    rows_all = grad_ref.shape[0]
    tiles = [pl.ds(8 * i, 8) for i in range(rows_all // 8)]
    for step in range(SWEEPS):
        c = jnp.broadcast_to(turn_ref[pl.ds(step, 1), :], (8, WIDTH))
        s = jnp.broadcast_to(turn_ref[pl.ds(SWEEPS + step, 1), :], (8, WIDTH))
        for i, rows in enumerate(tiles):
            low = pl.ds(rows_all + 8 * i, 8)
            if step == 0:
                if i % 2 == 0:
                    pair = grad_ref[pl.ds(8 * i, 16), :].astype(jnp.float32)
                half = pair[:8] if i % 2 == 0 else pair[8:]
                t, b = half[:, :WIDTH], half[:, WIDTH:]
            else:
                t, b = top_out[rows, :], bottom_out[rows, :]
            t, b = c * t + s * b, c * b - s * t
            b = pltpu.roll(b, WIDTH - 1, 1)
            top_out[rows, :] = t
            bottom_out[rows, :] = b
            if step == SWEEPS - 1:
                both_out[rows, :] = t
                both_out[low, :] = b


def cone_kernel(top0, pair1, pair2, bottom2, turn_out, blocks):
    count = ROOT_ROWS // 8
    per_group = HALO_ROWS // 8
    lane = lax.broadcasted_iota(jnp.int32, (8, LANES), 1)
    lane_group = lane // HALO
    homes = ((top0, 0), (pair1, 0), (pair2, 0), (pair1, CHUNK_ROWS), (pair2, CHUNK_ROWS), (bottom2, 0))

    def unfolded(places, i):
        g, q = divmod(i, per_group)
        out = None
        for p, (ref, first) in enumerate(places):
            piece = ref[pl.ds(first + ROOT_ROWS + 8 * q, 8), :]
            piece = pltpu.roll(piece, (p - g) * HALO % LANES, 1)
            out = piece if out is None else jnp.where(lane_group == p, piece, out)
        return out

    def given(index, i):
        rows = pl.ds(8 * i, 8)
        if index < 6:
            ref, first = homes[index]
            return ref[pl.ds(first + 8 * i, 8), :]
        return blocks[index, rows, :]

    for i in range(count):
        rows = pl.ds(8 * i, 8)
        blocks[6, rows, :] = unfolded(homes[:3], i)
        blocks[7, rows, :] = unfolded(homes[3:], i)

    def stored(index, i):
        return blocks[index, pl.ds(8 * i, 8), :]

    tt, bb, tb = ({} for _ in range(3))
    for p, (ti, bi) in enumerate(ROUND_PAIRS[0] + ((6, 4),)):
        acc = None
        for i in range(count):
            rows = pl.ds(8 * i, 8)
            t, b = given(ti, i), given(3 + bi, i)
            if p < 3:
                t, b = pltpu.roll(t, p * HALO, 1), pltpu.roll(b, p * HALO, 1)
                blocks[ti, rows, :] = t
                blocks[3 + bi, rows, :] = b
            acc = added(acc, b * b, t * b, t * t)
        bb[p], tb[p], tt[p] = (total8(x) for x in acc)

    steps = SWEEPS * len(ROUND_PAIRS)
    turns = {}

    def angles(n, p):
        if n >= steps:
            return
        cosine, sine, tt[p] = turn_of(tt[p], bb[p], tb[p])
        if p < 3:
            number, k = divmod(n, SWEEPS)
            row = SWEEPS * sum(len(q) for q in ROUND_PAIRS[:number]) + p * SWEEPS + k
            turn_out[0, pl.ds(row, 1), :] = cosine
            turn_out[0, pl.ds(STEPS + row, 1), :] = sine
        turns[p] = wide8(cosine), wide8(sine)

    def shift_of(n):
        return LANES - 1 - (HALO if n % SWEEPS == SWEEPS - 1 and n + 1 < steps else 0)

    def turn_halo(n):
        if n >= steps:
            return
        c, s = turns[3]
        acc = None
        for i in range(count):
            rows = pl.ds(8 * i, 8)
            t, b = stored(6, i), stored(7 + n % 3, i)
            t, b = c * t + s * b, c * b - s * t
            b = pltpu.roll(b, shift_of(n), 1)
            blocks[6, rows, :] = t
            blocks[7 + (n + 1) % 3, rows, :] = b
            acc = added(acc, b * b, t * b)
        bb[3], tb[3] = (total8(x) for x in acc)

    def turn_pair(n, p):
        number, k = divmod(n, SWEEPS)
        pairs = ROUND_PAIRS[number]
        ti, bi = pairs[p]
        ends = k + 1 == SWEEPS
        final = ends and number + 1 == len(ROUND_PAIRS)
        c, s = turns[p]
        need_top = not ends or p + 1 < len(pairs) or final
        need_bottom = not ends or p > 0 or final
        q = p - 1 if ends and not final else p
        by = shift_of(n)
        enters = lane == (q * HALO - 1) % LANES
        acc = None
        for i in range(count):
            rows = pl.ds(8 * i, 8)
            t, b = stored(ti, i), stored(3 + bi, i)
            top = c * t + s * b
            if need_top and not final:
                blocks[ti, rows, :] = top
            if need_bottom:
                entering = stored(7 + (n + 1) % 3, i)
                b = jnp.where(enters, entering, pltpu.roll(c * b - s * t, by, 1))
                if not final:
                    blocks[3 + bi, rows, :] = b
                other = top if q == p else stored(pairs[q][0], i)
                acc = added(acc, b * b, other * b)
        if need_bottom:
            bb[q], tb[q] = (total8(x) for x in acc)

    angles(0, 3)
    turn_halo(0)
    angles(1, 3)
    for n in range(steps):
        n_pairs = len(ROUND_PAIRS[n // SWEEPS])
        angles(n, 0)
        turn_halo(n + 1)
        for p in range(n_pairs):
            if p + 1 < n_pairs:
                angles(n, p + 1)
            if p == n_pairs - 1:
                angles(n + 2, 3)
            turn_pair(n, p)
    base = 0
    for pairs in ROUND_PAIRS:
        for p in range(len(pairs)):
            for first in (base, STEPS + base):
                rows = pl.ds(first + p * SWEEPS, SWEEPS)
                if p:
                    turn_out[0, rows, :] = pltpu.roll(turn_out[0, rows, :], LANES - p * HALO, 1)
        base += len(pairs) * SWEEPS
    turn_out[0, pl.ds(EIGEN_ROW, 1), :] = tt[0] * (1.0 / ROOT_ROWS)
    turn_out[0, pl.ds(EIGEN_ROW + 1, 1), :] = bb[0] * (1.0 / ROOT_ROWS)
    turn_out[0, pl.ds(EIGEN_ROW + 2, 6), :] = jnp.zeros((6, LANES), jnp.float32)
    for copy in range(1, PARTS):
        turn_out[copy] = turn_out[0]


def last_kernel(top0, pair1, pair2, bottom2, turns, eigen_out, projected_out, wide, blocks):
    rows_all = top0.shape[0]
    count = rows_all // 8
    for part in range(PARTS):
        wide[:, pl.ds(part * LANES, LANES)] = turns[part]

    def given(index, i):
        rows, low = pl.ds(8 * i, 8), pl.ds(rows_all + 8 * i, 8)
        return (
            lambda: top0[rows, :],
            lambda: pair1[rows, :],
            lambda: pair2[rows, :],
            lambda: pair1[low, :],
            lambda: pair2[low, :],
            lambda: bottom2[rows, :],
        )[index]()

    def row_of(row):
        return jnp.broadcast_to(wide[pl.ds(row, 1), :], (8, WIDTH))

    fresh = set()
    base = 0
    for number, pairs in enumerate(ROUND_PAIRS):
        final = number + 1 == len(ROUND_PAIRS)
        for k in range(SWEEPS):
            ends = k + 1 == SWEEPS
            for p, (ti, bi) in enumerate(pairs):
                c = row_of(base + p * SWEEPS + k)
                s = row_of(STEPS + base + p * SWEEPS + k)
                need_top = not ends or p + 1 < len(pairs) or final
                need_bottom = not ends or p > 0 or final
                for i in range(count):
                    rows = pl.ds(8 * i, 8)
                    t = blocks[ti, rows, :] if ti in fresh else given(ti, i)
                    b = blocks[3 + bi, rows, :] if 3 + bi in fresh else given(3 + bi, i)
                    if need_top:
                        top = c * t + s * b
                    if need_bottom:
                        bottom = c * b - s * t
                    if final and ends:
                        bottom = pltpu.roll(bottom, 4 * SWEEPS - 1, 1)
                        projected_out[rows, pl.ds(0, WIDTH)] = top * top
                        projected_out[rows, pl.ds(WIDTH, WIDTH)] = bottom * bottom
                        continue
                    if need_top:
                        blocks[ti, rows, :] = top
                    if need_bottom:
                        blocks[3 + bi, rows, :] = pltpu.roll(bottom, WIDTH - 1, 1)
                fresh |= {ti, 3 + bi}
        base += len(pairs) * SWEEPS
    eigen_out[pl.ds(0, WIDTH)] = wide[EIGEN_ROW, :]
    bottom = pltpu.roll(wide[pl.ds(EIGEN_ROW + 1, 1), :], 4 * SWEEPS, 1)
    eigen_out[pl.ds(WIDTH, WIDTH)] = bottom[0]


def call(kernel, outs, scratch, args, flops):
    f32 = jnp.float32
    vmem = pl.BlockSpec(memory_space=pltpu.VMEM)
    shapes = tuple(jax.ShapeDtypeStruct(shape, f32) for shape in outs)
    moved = sum(a.size * a.dtype.itemsize for a in args) + sum(4 * s.size for s in shapes)
    return pl.pallas_call(
        kernel,
        out_shape=shapes,
        in_specs=[vmem] * len(args),
        out_specs=tuple(vmem for _ in shapes),
        scratch_shapes=[pltpu.VMEM(shape, f32) for shape in scratch],
        compiler_params=pltpu.CompilerParams(vmem_limit_bytes=24 * MEGA),
        cost_estimate=pl.CostEstimate(flops=flops, bytes_accessed=moved, transcendentals=0),
    )(*args)


def from_slot(shard, offset):
    length = lax.axis_size("blk")
    return lax.ppermute(shard, "blk", [((i + offset) % length, i) for i in range(length)])


def body(root_rows, gradient):
    rows = gradient.shape[0]
    top_root, both_root, bottom_root, turn0 = call(
        first_kernel,
        [(CHUNK_ROWS, LANES), (2 * CHUNK_ROWS, LANES), (CHUNK_ROWS, LANES), (2 * SWEEPS, WIDTH)],
        [(ROOT_ROWS, WIDTH)] * 3,
        [root_rows],
        16 * ROOT_ROWS * WIDTH * SWEEPS,
    )
    root3 = from_slot(bottom_root, 3)
    root0 = from_slot(top_root, -3)
    root1 = from_slot(both_root, -1)
    root2 = from_slot(both_root, 1)
    top_grad, both_grad, bottom_grad = call(
        gradient_first_kernel,
        [(rows, WIDTH), (2 * rows, WIDTH), (rows, WIDTH)],
        [],
        [gradient, turn0],
        8 * rows * WIDTH * SWEEPS,
    )
    def after(value, *others):
        return lax.optimization_barrier((value, *others))[0]

    grad1 = from_slot(after(both_grad, root0), -1)
    grad2 = from_slot(after(both_grad, root3), 1)
    grad0 = from_slot(after(top_grad, root1), -3)
    grad3 = from_slot(after(bottom_grad, root2), 3)
    (turns,) = call(
        cone_kernel,
        [(PARTS, ANGLE_ROWS, LANES)],
        [(10, ROOT_ROWS, LANES)],
        [root0, root1, root2, root3],
        16 * CHUNK_ROWS * LANES * STEPS,
    )
    reps = lax.axis_size("rep")
    near = reps // PARTS
    groups = [[x * near + z for x in range(PARTS)] for z in range(near)]
    turns = lax.all_to_all(turns, "rep", 0, 0, axis_index_groups=groups)
    eigen, projected = call(
        last_kernel,
        [(2 * WIDTH,), (rows, 2 * WIDTH)],
        [(ANGLE_ROWS, WIDTH), (6, rows, WIDTH)],
        [grad0, grad1, grad2, grad3, turns],
        8 * rows * WIDTH * STEPS,
    )
    return eigen, projected


def solution(mesh):
    return jax.shard_map(
        body,
        mesh=mesh,
        in_specs=(P(None, "blk"), P("rep", "blk")),
        out_specs=(P("blk"), P("rep", "blk")),
        check_vma=False,
    )
```

```python
import functools
import jax
import jax.numpy as jnp
from jax import lax
from jax.experimental import pallas as pl
from jax.experimental.pallas import tpu as pltpu
from jax.sharding import PartitionSpec as P

ROOT_ROWS = 256
SWEEPS = 4
WIDTH = 512
LANES = 128
HALO = 16
GROUPS = LANES // HALO
HALO_ROWS = ROOT_ROWS // GROUPS
CHUNK_ROWS = ROOT_ROWS + HALO_ROWS
PARTS = WIDTH // LANES
ROUND_PAIRS = (((0, 0), (1, 1), (2, 2)), ((0, 1), (1, 2)), ((0, 2),))
STEPS = SWEEPS * sum(len(pairs) for pairs in ROUND_PAIRS)
EIGEN_ROW = 2 * STEPS
ANGLE_ROWS = 2 * STEPS + 8
MEGA = 1 << 20


def turn_of(tt, bb, tb):
    y = 2.0 * tb
    x = tt - bb
    ax = jnp.abs(x)
    ay = jnp.abs(y)
    top = jnp.maximum(ax, ay)
    none = top == 0.0
    scale = 1.0 / jnp.where(none, 1.0, top)
    xs = jnp.where(none, 1.0, ax * scale)
    ys = jnp.where(none, 0.0, ay * scale)
    squares = xs * xs + ys * ys
    inv = lax.rsqrt(squares)
    big = jnp.sqrt(0.5 + 0.5 * (xs * inv))
    small = 0.5 * (ys * inv) / big
    forward = x >= 0.0
    cosine = jnp.where(forward, big, small)
    size = jnp.where(forward, small, big)
    larger = 0.5 * (tt + bb) + 0.5 * (top * (squares * inv))
    return cosine, jnp.where(y < 0.0, -size, size), larger


def total8(acc):
    return jnp.sum(acc, axis=0, keepdims=True)


def added(acc, *new):
    return list(new) if acc is None else [x + y for x, y in zip(acc, new)]


def wide8(row):
    return jnp.broadcast_to(row, (8, LANES))


def even_slot():
    return lax.axis_index("blk") % 2 == 0


def first_kernel(root_ref, back_out, both_out, ahead_out, turn_out, top, bottom, rolled):
    tiles = [pl.ds(8 * i, 8) for i in range(ROOT_ROWS // 8)]
    cols = [pl.ds(g * LANES, LANES) for g in range(PARTS)]
    low_cols = [pl.ds(WIDTH + g * LANES, LANES) for g in range(PARTS)]
    last = lax.broadcasted_iota(jnp.int32, (8, LANES), 1) == LANES - 1
    tt, bb, tb = ([None] * PARTS for _ in range(3))
    for g in range(PARTS):
        acc = None
        for rows in tiles:
            t, b = root_ref[rows, cols[g]], root_ref[rows, low_cols[g]]
            acc = added(acc, b * b, t * b, t * t)
        bb[g], tb[g], tt[g] = (total8(x) for x in acc)

    def rotate(step, g):
        cosine, sine, tt[g] = turn_of(tt[g], bb[g], tb[g])
        turn_out[pl.ds(step, 1), cols[g]] = cosine
        turn_out[pl.ds(SWEEPS + step, 1), cols[g]] = sine
        c, s = wide8(cosine), wide8(sine)
        for rows in tiles:
            if step == 0:
                t, b = root_ref[rows, cols[g]], root_ref[rows, low_cols[g]]
            else:
                t, b = top[rows, cols[g]], bottom[rows, cols[g]]
            top[rows, cols[g]] = c * t + s * b
            rolled[rows, cols[g]] = pltpu.roll(c * b - s * t, LANES - 1, 1)

    def shift(step, g):
        acc = None
        for rows in tiles:
            b = jnp.where(last, rolled[rows, cols[(g + 1) % PARTS]], rolled[rows, cols[g]])
            bottom[rows, cols[g]] = b
            if step + 1 < SWEEPS:
                acc = added(acc, b * b, top[rows, cols[g]] * b)
        if step + 1 < SWEEPS:
            bb[g], tb[g] = (total8(x) for x in acc)

    for step in range(SWEEPS):
        rotate(step, 0)
        for g in range(1, PARTS):
            rotate(step, g)
            shift(step, g - 1)
        shift(step, PARTS - 1)

    part = lax.axis_index("rep") // PARTS
    here = pl.ds(pl.multiple_of(part * LANES, LANES), LANES)
    after = pl.ds(pl.multiple_of(lax.rem(part + 1, PARTS) * LANES, LANES), LANES)
    lane_group = lax.broadcasted_iota(jnp.int32, (8, LANES), 1) // HALO

    def folded(block, q):
        out = block[pl.ds(8 * q, 8), after]
        for g in range(1, GROUPS):
            piece = block[pl.ds(g * HALO_ROWS + 8 * q, 8), after]
            out = jnp.where(lane_group == g, pltpu.roll(piece, g * HALO, 1), out)
        return out

    even = even_slot()
    for v in range(CHUNK_ROWS // 8):
        if v < ROOT_ROWS // 8:
            t, b = top[pl.ds(8 * v, 8), here], bottom[pl.ds(8 * v, 8), here]
        else:
            t, b = (folded(block, v - ROOT_ROWS // 8) for block in (top, bottom))
        both_out[pl.ds(8 * v, 8), :] = t
        both_out[pl.ds(CHUNK_ROWS + 8 * v, 8), :] = b
        back_out[pl.ds(8 * v, 8), :] = jnp.where(even, b, t)
        ahead_out[pl.ds(8 * v, 8), :] = jnp.where(even, t, b)


def gradient_first_kernel(grad_ref, turn_ref, back_out, both_out, ahead_out):
    even = even_slot()
    rows_all = grad_ref.shape[0]
    tiles = [pl.ds(8 * i, 8) for i in range(rows_all // 8)]
    for step in range(SWEEPS):
        c = jnp.broadcast_to(turn_ref[pl.ds(step, 1), :], (8, WIDTH))
        s = jnp.broadcast_to(turn_ref[pl.ds(SWEEPS + step, 1), :], (8, WIDTH))
        for i, rows in enumerate(tiles):
            low = pl.ds(rows_all + 8 * i, 8)
            if step == 0:
                if i % 2 == 0:
                    pair = grad_ref[pl.ds(8 * i, 16), :].astype(jnp.float32)
                half = pair[:8] if i % 2 == 0 else pair[8:]
                t, b = half[:, :WIDTH], half[:, WIDTH:]
            else:
                t, b = both_out[rows, :], both_out[low, :]
            t, b = c * t + s * b, c * b - s * t
            b = pltpu.roll(b, WIDTH - 1, 1)
            both_out[rows, :] = t
            both_out[low, :] = b
            if step == SWEEPS - 1:
                back_out[rows, :] = jnp.where(even, b, t)
                ahead_out[rows, :] = jnp.where(even, t, b)


def cone_kernel(back, pair_out, pair_in, ahead, turn_out, blocks):
    count = ROOT_ROWS // 8
    per_group = HALO_ROWS // 8
    lane = lax.broadcasted_iota(jnp.int32, (8, LANES), 1)
    lane_group = lane // HALO
    even = even_slot()
    homes = (
        (back, ahead, 0),
        (pair_out, pair_in, 0),
        (pair_in, pair_out, 0),
        (pair_out, pair_in, CHUNK_ROWS),
        (pair_in, pair_out, CHUNK_ROWS),
        (ahead, back, 0),
    )

    def home(index, row):
        on_even, on_odd, first = homes[index]
        rows = pl.ds(first + row, 8)
        return jnp.where(even, on_even[rows, :], on_odd[rows, :])

    def unfolded(places, i):
        g, q = divmod(i, per_group)
        out = None
        for p, index in enumerate(places):
            piece = home(index, ROOT_ROWS + 8 * q)
            piece = pltpu.roll(piece, (p - g) * HALO % LANES, 1)
            out = piece if out is None else jnp.where(lane_group == p, piece, out)
        return out

    def given(index, i):
        return home(index, 8 * i) if index < 6 else blocks[index, pl.ds(8 * i, 8), :]

    for i in range(count):
        rows = pl.ds(8 * i, 8)
        blocks[6, rows, :] = unfolded((0, 1, 2), i)
        blocks[7, rows, :] = unfolded((3, 4, 5), i)

    def stored(index, i):
        return blocks[index, pl.ds(8 * i, 8), :]

    tt, bb, tb = ({} for _ in range(3))
    for p, (ti, bi) in enumerate(ROUND_PAIRS[0] + ((6, 4),)):
        acc = None
        for i in range(count):
            rows = pl.ds(8 * i, 8)
            t, b = given(ti, i), given(3 + bi, i)
            if p < 3:
                t, b = pltpu.roll(t, p * HALO, 1), pltpu.roll(b, p * HALO, 1)
                blocks[ti, rows, :] = t
                blocks[3 + bi, rows, :] = b
            acc = added(acc, b * b, t * b, t * t)
        bb[p], tb[p], tt[p] = (total8(x) for x in acc)

    steps = SWEEPS * len(ROUND_PAIRS)
    turns = {}

    def angles(n, p):
        if n >= steps:
            return
        cosine, sine, tt[p] = turn_of(tt[p], bb[p], tb[p])
        if p < 3:
            number, k = divmod(n, SWEEPS)
            row = SWEEPS * sum(len(q) for q in ROUND_PAIRS[:number]) + p * SWEEPS + k
            turn_out[0, pl.ds(row, 1), :] = cosine
            turn_out[0, pl.ds(STEPS + row, 1), :] = sine
        turns[p] = wide8(cosine), wide8(sine)

    def shift_of(n):
        return LANES - 1 - (HALO if n % SWEEPS == SWEEPS - 1 and n + 1 < steps else 0)

    def turn_halo(n):
        if n >= steps:
            return
        c, s = turns[3]
        acc = None
        for i in range(count):
            rows = pl.ds(8 * i, 8)
            t, b = stored(6, i), stored(7 + n % 3, i)
            t, b = c * t + s * b, c * b - s * t
            b = pltpu.roll(b, shift_of(n), 1)
            blocks[6, rows, :] = t
            blocks[7 + (n + 1) % 3, rows, :] = b
            acc = added(acc, b * b, t * b)
        bb[3], tb[3] = (total8(x) for x in acc)

    def turn_pair(n, p):
        number, k = divmod(n, SWEEPS)
        pairs = ROUND_PAIRS[number]
        ti, bi = pairs[p]
        ends = k + 1 == SWEEPS
        final = ends and number + 1 == len(ROUND_PAIRS)
        c, s = turns[p]
        need_top = not ends or p + 1 < len(pairs) or final
        need_bottom = not ends or p > 0 or final
        q = p - 1 if ends and not final else p
        by = shift_of(n)
        enters = lane == (q * HALO - 1) % LANES
        acc = None
        for i in range(count):
            rows = pl.ds(8 * i, 8)
            t, b = stored(ti, i), stored(3 + bi, i)
            top = c * t + s * b
            if need_top and not final:
                blocks[ti, rows, :] = top
            if need_bottom:
                entering = stored(7 + (n + 1) % 3, i)
                b = jnp.where(enters, entering, pltpu.roll(c * b - s * t, by, 1))
                if not final:
                    blocks[3 + bi, rows, :] = b
                other = top if q == p else stored(pairs[q][0], i)
                acc = added(acc, b * b, other * b)
        if need_bottom:
            bb[q], tb[q] = (total8(x) for x in acc)

    angles(0, 3)
    turn_halo(0)
    angles(1, 3)
    for n in range(steps):
        n_pairs = len(ROUND_PAIRS[n // SWEEPS])
        angles(n, 0)
        turn_halo(n + 1)
        for p in range(n_pairs):
            if p + 1 < n_pairs:
                angles(n, p + 1)
            if p == n_pairs - 1:
                angles(n + 2, 3)
            turn_pair(n, p)
    base = 0
    for pairs in ROUND_PAIRS:
        for p in range(len(pairs)):
            for first in (base, STEPS + base):
                rows = pl.ds(first + p * SWEEPS, SWEEPS)
                if p:
                    turn_out[0, rows, :] = pltpu.roll(turn_out[0, rows, :], LANES - p * HALO, 1)
        base += len(pairs) * SWEEPS
    turn_out[0, pl.ds(EIGEN_ROW, 1), :] = tt[0] * (1.0 / ROOT_ROWS)
    turn_out[0, pl.ds(EIGEN_ROW + 1, 1), :] = bb[0] * (1.0 / ROOT_ROWS)
    turn_out[0, pl.ds(EIGEN_ROW + 2, 6), :] = jnp.zeros((6, LANES), jnp.float32)
    for copy in range(1, PARTS):
        turn_out[copy] = turn_out[0]


def last_kernel(back, pair_out, pair_in, ahead, turns, eigen_out, projected_out, wide, blocks):
    rows_all = back.shape[0]
    even = even_slot()
    count = rows_all // 8
    for part in range(PARTS):
        wide[:, pl.ds(part * LANES, LANES)] = turns[part]

    def given(index, i):
        on_even, on_odd, first = (
            (back, ahead, 0),
            (pair_out, pair_in, 0),
            (pair_in, pair_out, 0),
            (pair_out, pair_in, rows_all),
            (pair_in, pair_out, rows_all),
            (ahead, back, 0),
        )[index]
        rows = pl.ds(first + 8 * i, 8)
        return jnp.where(even, on_even[rows, :], on_odd[rows, :])

    def row_of(row):
        return jnp.broadcast_to(wide[pl.ds(row, 1), :], (8, WIDTH))

    fresh = set()
    base = 0
    for number, pairs in enumerate(ROUND_PAIRS):
        final = number + 1 == len(ROUND_PAIRS)
        for k in range(SWEEPS):
            ends = k + 1 == SWEEPS
            for p, (ti, bi) in enumerate(pairs):
                c = row_of(base + p * SWEEPS + k)
                s = row_of(STEPS + base + p * SWEEPS + k)
                need_top = not ends or p + 1 < len(pairs) or final
                need_bottom = not ends or p > 0 or final
                for i in range(count):
                    rows = pl.ds(8 * i, 8)
                    t = blocks[ti, rows, :] if ti in fresh else given(ti, i)
                    b = blocks[3 + bi, rows, :] if 3 + bi in fresh else given(3 + bi, i)
                    if need_top:
                        top = c * t + s * b
                    if need_bottom:
                        bottom = c * b - s * t
                    if final and ends:
                        bottom = pltpu.roll(bottom, 4 * SWEEPS - 1, 1)
                        projected_out[rows, pl.ds(0, WIDTH)] = top * top
                        projected_out[rows, pl.ds(WIDTH, WIDTH)] = bottom * bottom
                        continue
                    if need_top:
                        blocks[ti, rows, :] = top
                    if need_bottom:
                        blocks[3 + bi, rows, :] = pltpu.roll(bottom, WIDTH - 1, 1)
                fresh |= {ti, 3 + bi}
        base += len(pairs) * SWEEPS
    eigen_out[pl.ds(0, WIDTH)] = wide[EIGEN_ROW, :]
    bottom = pltpu.roll(wide[pl.ds(EIGEN_ROW + 1, 1), :], 4 * SWEEPS, 1)
    eigen_out[pl.ds(WIDTH, WIDTH)] = bottom[0]


def call(kernel, outs, scratch, args, flops):
    f32 = jnp.float32
    vmem = pl.BlockSpec(memory_space=pltpu.VMEM)
    shapes = tuple(jax.ShapeDtypeStruct(shape, f32) for shape in outs)
    moved = sum(a.size * a.dtype.itemsize for a in args) + sum(4 * s.size for s in shapes)
    return pl.pallas_call(
        kernel,
        out_shape=shapes,
        in_specs=[vmem] * len(args),
        out_specs=tuple(vmem for _ in shapes),
        scratch_shapes=[pltpu.VMEM(shape, f32) for shape in scratch],
        compiler_params=pltpu.CompilerParams(vmem_limit_bytes=24 * MEGA),
        cost_estimate=pl.CostEstimate(flops=flops, bytes_accessed=moved, transcendentals=0),
    )(*args)


def swapped(shard, by):
    length = lax.axis_size("blk")
    return lax.ppermute(
        shard, "blk", [((i + (by if i % 2 == 0 else -by)) % length, i) for i in range(length)]
    )


def body(root_rows, gradient):
    rows = gradient.shape[0]
    back_root, both_root, ahead_root, turn0 = call(
        first_kernel,
        [(CHUNK_ROWS, LANES), (2 * CHUNK_ROWS, LANES), (CHUNK_ROWS, LANES), (2 * SWEEPS, WIDTH)],
        [(ROOT_ROWS, WIDTH)] * 3,
        [root_rows],
        16 * ROOT_ROWS * WIDTH * SWEEPS,
    )
    root3 = swapped(ahead_root, 3)
    root0 = swapped(back_root, -3)
    root1 = swapped(both_root, -1)
    root2 = swapped(both_root, 1)
    back_grad, both_grad, ahead_grad = call(
        gradient_first_kernel,
        [(rows, WIDTH), (2 * rows, WIDTH), (rows, WIDTH)],
        [],
        [gradient, turn0],
        8 * rows * WIDTH * SWEEPS,
    )
    def after(value, *others):
        return lax.optimization_barrier((value, *others))[0]

    grad1 = swapped(after(both_grad, root0), -1)
    grad2 = swapped(after(both_grad, root3), 1)
    grad0 = swapped(after(back_grad, root1), -3)
    grad3 = swapped(after(ahead_grad, root2), 3)
    (turns,) = call(
        cone_kernel,
        [(PARTS, ANGLE_ROWS, LANES)],
        [(10, ROOT_ROWS, LANES)],
        [root0, root1, root2, root3],
        16 * CHUNK_ROWS * LANES * STEPS,
    )
    reps = lax.axis_size("rep")
    near = reps // PARTS
    groups = [[x * near + z for x in range(PARTS)] for z in range(near)]
    turns = lax.all_to_all(turns, "rep", 0, 0, axis_index_groups=groups)
    eigen, projected = call(
        last_kernel,
        [(2 * WIDTH,), (rows, 2 * WIDTH)],
        [(ANGLE_ROWS, WIDTH), (6, rows, WIDTH)],
        [grad0, grad1, grad2, grad3, turns],
        8 * rows * WIDTH * STEPS,
    )
    return eigen, projected


def solution(mesh):
    return jax.shard_map(
        body,
        mesh=mesh,
        in_specs=(P(None, "blk"), P("rep", "blk")),
        out_specs=(P("blk"), P("rep", "blk")),
        check_vma=False,
    )
```

```python
import functools
import jax
import jax.numpy as jnp
from jax import lax
from jax.experimental import pallas as pl
from jax.experimental.pallas import tpu as pltpu
from jax.sharding import PartitionSpec as P

ROOT_ROWS = 256
SWEEPS = 4
WIDTH = 512
LANES = 128
HALO = 16
GROUPS = LANES // HALO
HALO_ROWS = ROOT_ROWS // GROUPS
CHUNK_ROWS = ROOT_ROWS + HALO_ROWS
PARTS = WIDTH // LANES
ROUND_PAIRS = (((0, 0), (1, 1), (2, 2)), ((0, 1), (1, 2)), ((0, 2),))
STEPS = SWEEPS * sum(len(pairs) for pairs in ROUND_PAIRS)
EIGEN_ROW = 2 * STEPS
ANGLE_ROWS = 2 * STEPS + 8
MEGA = 1 << 20


def turn_of(tt, bb, tb):
    y = 2.0 * tb
    x = tt - bb
    ax = jnp.abs(x)
    ay = jnp.abs(y)
    top = jnp.maximum(ax, ay)
    none = top == 0.0
    scale = 1.0 / jnp.where(none, 1.0, top)
    xs = jnp.where(none, 1.0, ax * scale)
    ys = jnp.where(none, 0.0, ay * scale)
    squares = xs * xs + ys * ys
    inv = lax.rsqrt(squares)
    big = jnp.sqrt(0.5 + 0.5 * (xs * inv))
    small = 0.5 * (ys * inv) / big
    forward = x >= 0.0
    cosine = jnp.where(forward, big, small)
    size = jnp.where(forward, small, big)
    larger = 0.5 * (tt + bb) + 0.5 * (top * (squares * inv))
    return cosine, jnp.where(y < 0.0, -size, size), larger


def total8(acc):
    return jnp.sum(acc, axis=0, keepdims=True)


def added(acc, *new):
    return list(new) if acc is None else [x + y for x, y in zip(acc, new)]


def wide8(row):
    return jnp.broadcast_to(row, (8, LANES))


def even_slot():
    return lax.axis_index("blk") % 2 == 0


def first_kernel(root_ref, back_out, both_out, ahead_out, turn_out, top, bottom, rolled):
    tiles = [pl.ds(8 * i, 8) for i in range(ROOT_ROWS // 8)]
    cols = [pl.ds(g * LANES, LANES) for g in range(PARTS)]
    low_cols = [pl.ds(WIDTH + g * LANES, LANES) for g in range(PARTS)]
    last = lax.broadcasted_iota(jnp.int32, (8, LANES), 1) == LANES - 1
    tt, bb, tb = ([None] * PARTS for _ in range(3))
    for g in range(PARTS):
        acc = None
        for rows in tiles:
            t, b = root_ref[rows, cols[g]], root_ref[rows, low_cols[g]]
            acc = added(acc, b * b, t * b, t * t)
        bb[g], tb[g], tt[g] = (total8(x) for x in acc)

    def rotate(step, g):
        cosine, sine, tt[g] = turn_of(tt[g], bb[g], tb[g])
        turn_out[pl.ds(step, 1), cols[g]] = cosine
        turn_out[pl.ds(SWEEPS + step, 1), cols[g]] = sine
        c, s = wide8(cosine), wide8(sine)
        for rows in tiles:
            if step == 0:
                t, b = root_ref[rows, cols[g]], root_ref[rows, low_cols[g]]
            else:
                t, b = top[rows, cols[g]], bottom[rows, cols[g]]
            top[rows, cols[g]] = c * t + s * b
            rolled[rows, cols[g]] = pltpu.roll(c * b - s * t, LANES - 1, 1)

    def shift(step, g):
        acc = None
        for rows in tiles:
            b = jnp.where(last, rolled[rows, cols[(g + 1) % PARTS]], rolled[rows, cols[g]])
            bottom[rows, cols[g]] = b
            if step + 1 < SWEEPS:
                acc = added(acc, b * b, top[rows, cols[g]] * b)
        if step + 1 < SWEEPS:
            bb[g], tb[g] = (total8(x) for x in acc)

    for step in range(SWEEPS):
        rotate(step, 0)
        for g in range(1, PARTS):
            rotate(step, g)
            shift(step, g - 1)
        shift(step, PARTS - 1)

    part = lax.axis_index("rep") // PARTS
    here = pl.ds(pl.multiple_of(part * LANES, LANES), LANES)
    after = pl.ds(pl.multiple_of(lax.rem(part + 1, PARTS) * LANES, LANES), LANES)
    lane_group = lax.broadcasted_iota(jnp.int32, (8, LANES), 1) // HALO

    def folded(block, q):
        out = block[pl.ds(8 * q, 8), after]
        for g in range(1, GROUPS):
            piece = block[pl.ds(g * HALO_ROWS + 8 * q, 8), after]
            out = jnp.where(lane_group == g, pltpu.roll(piece, g * HALO, 1), out)
        return out

    even = even_slot()
    for v in range(CHUNK_ROWS // 8):
        if v < ROOT_ROWS // 8:
            t, b = top[pl.ds(8 * v, 8), here], bottom[pl.ds(8 * v, 8), here]
        else:
            t, b = (folded(block, v - ROOT_ROWS // 8) for block in (top, bottom))
        both_out[pl.ds(8 * v, 8), :] = t
        both_out[pl.ds(CHUNK_ROWS + 8 * v, 8), :] = b
        back_out[pl.ds(8 * v, 8), :] = jnp.where(even, b, t)
        ahead_out[pl.ds(8 * v, 8), :] = jnp.where(even, t, b)


def gradient_first_kernel(grad_ref, turn_ref, back_out, both_out, ahead_out):
    even = even_slot()
    rows_all = grad_ref.shape[0]
    tiles = [pl.ds(8 * i, 8) for i in range(rows_all // 8)]
    for step in range(SWEEPS):
        c = jnp.broadcast_to(turn_ref[pl.ds(step, 1), :], (8, WIDTH))
        s = jnp.broadcast_to(turn_ref[pl.ds(SWEEPS + step, 1), :], (8, WIDTH))
        for i, rows in enumerate(tiles):
            low = pl.ds(rows_all + 8 * i, 8)
            if step == 0:
                if i % 2 == 0:
                    pair = grad_ref[pl.ds(8 * i, 16), :].astype(jnp.float32)
                half = pair[:8] if i % 2 == 0 else pair[8:]
                t, b = half[:, :WIDTH], half[:, WIDTH:]
            else:
                t, b = both_out[rows, :], both_out[low, :]
            t, b = c * t + s * b, c * b - s * t
            b = pltpu.roll(b, WIDTH - 1, 1)
            both_out[rows, :] = t
            both_out[low, :] = b
            if step == SWEEPS - 1:
                back_out[rows, :] = jnp.where(even, b, t)
                ahead_out[rows, :] = jnp.where(even, t, b)


def cone_kernel(back, pair_out, pair_in, ahead, turn_out, blocks):
    count = ROOT_ROWS // 8
    per_group = HALO_ROWS // 8
    lane = lax.broadcasted_iota(jnp.int32, (8, LANES), 1)
    lane_group = lane // HALO
    even = even_slot()
    homes = (
        (back, ahead, 0),
        (pair_out, pair_in, 0),
        (pair_in, pair_out, 0),
        (pair_out, pair_in, CHUNK_ROWS),
        (pair_in, pair_out, CHUNK_ROWS),
        (ahead, back, 0),
    )

    def home(index, row):
        on_even, on_odd, first = homes[index]
        rows = pl.ds(first + row, 8)
        return jnp.where(even, on_even[rows, :], on_odd[rows, :])

    def unfolded(places, i):
        g, q = divmod(i, per_group)
        out = None
        for p, index in enumerate(places):
            piece = home(index, ROOT_ROWS + 8 * q)
            piece = pltpu.roll(piece, (p - g) * HALO % LANES, 1)
            out = piece if out is None else jnp.where(lane_group == p, piece, out)
        return out

    def given(index, i):
        return home(index, 8 * i) if index < 6 else blocks[index, pl.ds(8 * i, 8), :]

    for i in range(count):
        rows = pl.ds(8 * i, 8)
        blocks[6, rows, :] = unfolded((0, 1, 2), i)
        blocks[7, rows, :] = unfolded((3, 4, 5), i)

    def stored(index, i):
        return blocks[index, pl.ds(8 * i, 8), :]

    tt, bb, tb = ({} for _ in range(3))
    for p, (ti, bi) in enumerate(ROUND_PAIRS[0] + ((6, 4),)):
        acc = None
        for i in range(count):
            rows = pl.ds(8 * i, 8)
            t, b = given(ti, i), given(3 + bi, i)
            if p < 3:
                t, b = pltpu.roll(t, p * HALO, 1), pltpu.roll(b, p * HALO, 1)
                blocks[ti, rows, :] = t
                blocks[3 + bi, rows, :] = b
            acc = added(acc, b * b, t * b, t * t)
        bb[p], tb[p], tt[p] = (total8(x) for x in acc)

    steps = SWEEPS * len(ROUND_PAIRS)
    turns = {}

    def angles(n, p):
        if n >= steps:
            return
        cosine, sine, tt[p] = turn_of(tt[p], bb[p], tb[p])
        if p < 3:
            number, k = divmod(n, SWEEPS)
            row = SWEEPS * sum(len(q) for q in ROUND_PAIRS[:number]) + p * SWEEPS + k
            turn_out[0, pl.ds(row, 1), :] = cosine
            turn_out[0, pl.ds(STEPS + row, 1), :] = sine
        turns[p] = wide8(cosine), wide8(sine)

    def shift_of(n):
        return LANES - 1 - (HALO if n % SWEEPS == SWEEPS - 1 and n + 1 < steps else 0)

    def turn_halo(n):
        if n >= steps:
            return
        c, s = turns[3]
        acc = None
        for i in range(count):
            rows = pl.ds(8 * i, 8)
            t, b = stored(6, i), stored(7 + n % 3, i)
            t, b = c * t + s * b, c * b - s * t
            b = pltpu.roll(b, shift_of(n), 1)
            blocks[6, rows, :] = t
            blocks[7 + (n + 1) % 3, rows, :] = b
            acc = added(acc, b * b, t * b)
        bb[3], tb[3] = (total8(x) for x in acc)

    def turn_pair(n, p):
        number, k = divmod(n, SWEEPS)
        pairs = ROUND_PAIRS[number]
        ti, bi = pairs[p]
        ends = k + 1 == SWEEPS
        final = ends and number + 1 == len(ROUND_PAIRS)
        c, s = turns[p]
        need_top = not ends or p + 1 < len(pairs) or final
        need_bottom = not ends or p > 0 or final
        q = p - 1 if ends and not final else p
        by = shift_of(n)
        enters = lane == (q * HALO - 1) % LANES
        acc = None
        for i in range(count):
            rows = pl.ds(8 * i, 8)
            t, b = stored(ti, i), stored(3 + bi, i)
            top = c * t + s * b
            if need_top and not final:
                blocks[ti, rows, :] = top
            if need_bottom:
                entering = stored(7 + (n + 1) % 3, i)
                b = jnp.where(enters, entering, pltpu.roll(c * b - s * t, by, 1))
                if not final:
                    blocks[3 + bi, rows, :] = b
                other = top if q == p else stored(pairs[q][0], i)
                acc = added(acc, b * b, other * b)
        if need_bottom:
            bb[q], tb[q] = (total8(x) for x in acc)

    angles(0, 3)
    turn_halo(0)
    angles(1, 3)
    for n in range(steps):
        n_pairs = len(ROUND_PAIRS[n // SWEEPS])
        angles(n, 0)
        turn_halo(n + 1)
        for p in range(n_pairs):
            if p + 1 < n_pairs:
                angles(n, p + 1)
            if p == n_pairs - 1:
                angles(n + 2, 3)
            turn_pair(n, p)
    base = 0
    for pairs in ROUND_PAIRS:
        for p in range(len(pairs)):
            for first in (base, STEPS + base):
                rows = pl.ds(first + p * SWEEPS, SWEEPS)
                if p:
                    turn_out[0, rows, :] = pltpu.roll(turn_out[0, rows, :], LANES - p * HALO, 1)
        base += len(pairs) * SWEEPS
    turn_out[0, pl.ds(EIGEN_ROW, 1), :] = tt[0] * (1.0 / ROOT_ROWS)
    turn_out[0, pl.ds(EIGEN_ROW + 1, 1), :] = bb[0] * (1.0 / ROOT_ROWS)
    turn_out[0, pl.ds(EIGEN_ROW + 2, 6), :] = jnp.zeros((6, LANES), jnp.float32)
    for copy in range(1, PARTS):
        turn_out[copy] = turn_out[0]


def widened(turns, wide):
    for part in range(PARTS):
        wide[:, pl.ds(part * LANES, LANES)] = turns[part]


def turned_pair(wide, row, source, target, count, finish):
    for k in range(SWEEPS):
        c = jnp.broadcast_to(wide[pl.ds(row + k, 1), :], (8, WIDTH))
        s = jnp.broadcast_to(wide[pl.ds(STEPS + row + k, 1), :], (8, WIDTH))
        for i in range(count):
            rows = pl.ds(8 * i, 8)
            t, b = source(i) if k == 0 else (target[0][rows, :], target[1][rows, :])
            t, b = c * t + s * b, c * b - s * t
            if k + 1 == SWEEPS:
                finish(i, t, b)
            else:
                target[0][rows, :] = t
                target[1][rows, :] = pltpu.roll(b, WIDTH - 1, 1)


def row_of(pair_round, even_pair, odd_pair):
    base = SWEEPS * sum(len(pairs) for pairs in ROUND_PAIRS[:pair_round])
    return jnp.where(even_slot(), base + SWEEPS * even_pair, base + SWEEPS * odd_pair)


def middle_kernel(back, pair_out, pair_in, turns, eigen_out, near_out, done_out, wide, t0, b0, t1, b1):
    rows_all = back.shape[0]
    count = rows_all // 8
    even = even_slot()
    widened(turns, wide)

    def parts(i):
        rows, low = pl.ds(8 * i, 8), pl.ds(rows_all + 8 * i, 8)
        return rows, low

    def outer(i):
        rows, low = parts(i)
        far = back[rows, :]
        return jnp.where(even, far, pair_out[rows, :]), jnp.where(even, pair_out[low, :], far)

    def inner(i):
        rows, low = parts(i)
        return (
            jnp.where(even, pair_out[rows, :], pair_in[rows, :]),
            jnp.where(even, pair_in[low, :], pair_out[low, :]),
        )

    def keep_outer(i, t, b):
        t0[parts(i)[0], :] = jnp.where(even, t, pltpu.roll(b, WIDTH - 1, 1))

    def keep_inner(i, t, b):
        rows = parts(i)[0]
        t1[rows, :] = t
        b1[rows, :] = pltpu.roll(b, WIDTH - 1, 1)
        near_out[rows, :] = jnp.where(even, t, b1[rows, :])

    def second(i):
        rows = parts(i)[0]
        kept = t0[rows, :]
        return jnp.where(even, kept, t1[rows, :]), jnp.where(even, b1[rows, :], kept)

    def keep_second(i, t, b):
        done_out[parts(i)[0], :] = jnp.where(even, t, pltpu.roll(b, WIDTH - 1, 1))

    turned_pair(wide, row_of(0, 0, 2), outer, (t0, b0), count, keep_outer)
    turned_pair(wide, row_of(0, 1, 1), inner, (t1, b1), count, keep_inner)
    turned_pair(wide, row_of(1, 0, 1), second, (t1, b1), count, keep_second)

    eigen_out[pl.ds(0, WIDTH)] = wide[EIGEN_ROW, :]
    bottom = pltpu.roll(wide[pl.ds(EIGEN_ROW + 1, 1), :], 4 * SWEEPS, 1)
    eigen_out[pl.ds(WIDTH, WIDTH)] = bottom[0]


def last_kernel(pair_in, ahead, near, done, turns, projected_out, wide, t0, b0):
    rows_all = ahead.shape[0]
    count = rows_all // 8
    even = even_slot()
    widened(turns, wide)

    def first(i):
        rows, low = pl.ds(8 * i, 8), pl.ds(rows_all + 8 * i, 8)
        far = ahead[rows, :]
        return jnp.where(even, pair_in[rows, :], far), jnp.where(even, far, pair_in[low, :])

    def keep(i, t, b):
        t0[pl.ds(8 * i, 8), :] = jnp.where(even, pltpu.roll(b, WIDTH - 1, 1), t)

    def with_kept(other):
        def source(i):
            rows = pl.ds(8 * i, 8)
            kept, held = t0[rows, :], other[rows, :]
            return jnp.where(even, held, kept), jnp.where(even, kept, held)

        return source

    def write(i, t, b):
        rows = pl.ds(8 * i, 8)
        b = pltpu.roll(b, 4 * SWEEPS - 1, 1)
        projected_out[rows, pl.ds(0, WIDTH)] = t * t
        projected_out[rows, pl.ds(WIDTH, WIDTH)] = b * b

    turned_pair(wide, row_of(0, 2, 0), first, (t0, b0), count, keep)
    turned_pair(wide, row_of(1, 1, 0), with_kept(near), (t0, b0), count, keep)
    turned_pair(wide, row_of(2, 0, 0), with_kept(done), (t0, b0), count, write)


def call(kernel, outs, scratch, args, flops):
    f32 = jnp.float32
    vmem = pl.BlockSpec(memory_space=pltpu.VMEM)
    shapes = tuple(jax.ShapeDtypeStruct(shape, f32) for shape in outs)
    moved = sum(a.size * a.dtype.itemsize for a in args) + sum(4 * s.size for s in shapes)
    return pl.pallas_call(
        kernel,
        out_shape=shapes,
        in_specs=[vmem] * len(args),
        out_specs=tuple(vmem for _ in shapes),
        scratch_shapes=[pltpu.VMEM(shape, f32) for shape in scratch],
        compiler_params=pltpu.CompilerParams(vmem_limit_bytes=24 * MEGA),
        cost_estimate=pl.CostEstimate(flops=flops, bytes_accessed=moved, transcendentals=0),
    )(*args)


def swapped(shard, by):
    length = lax.axis_size("blk")
    return lax.ppermute(
        shard, "blk", [((i + (by if i % 2 == 0 else -by)) % length, i) for i in range(length)]
    )


def body(root_rows, gradient):
    rows = gradient.shape[0]
    back_root, both_root, ahead_root, turn0 = call(
        first_kernel,
        [(CHUNK_ROWS, LANES), (2 * CHUNK_ROWS, LANES), (CHUNK_ROWS, LANES), (2 * SWEEPS, WIDTH)],
        [(ROOT_ROWS, WIDTH)] * 3,
        [root_rows],
        16 * ROOT_ROWS * WIDTH * SWEEPS,
    )
    root3 = swapped(ahead_root, 3)
    root0 = swapped(back_root, -3)
    root1 = swapped(both_root, -1)
    root2 = swapped(both_root, 1)
    back_grad, both_grad, ahead_grad = call(
        gradient_first_kernel,
        [(rows, WIDTH), (2 * rows, WIDTH), (rows, WIDTH)],
        [],
        [gradient, turn0],
        8 * rows * WIDTH * SWEEPS,
    )
    def after(value, *others):
        return lax.optimization_barrier((value, *others))[0]

    grad1 = swapped(after(both_grad, root0), -1)
    grad2 = swapped(after(both_grad, root3), 1)
    grad0 = swapped(after(back_grad, root1), -3)
    grad3 = swapped(after(ahead_grad, root2), 3)
    (turns,) = call(
        cone_kernel,
        [(PARTS, ANGLE_ROWS, LANES)],
        [(10, ROOT_ROWS, LANES)],
        [root0, root1, root2, root3],
        16 * CHUNK_ROWS * LANES * STEPS,
    )
    reps = lax.axis_size("rep")
    near = reps // PARTS
    groups = [[x * near + z for x in range(PARTS)] for z in range(near)]
    turns = lax.all_to_all(turns, "rep", 0, 0, axis_index_groups=groups)
    block, angles = (rows, WIDTH), (ANGLE_ROWS, WIDTH)
    eigen, near_block, done_block = call(
        middle_kernel,
        [(2 * WIDTH,), block, block],
        [angles] + [block] * 4,
        [grad0, grad1, grad2, turns],
        4 * rows * WIDTH * STEPS,
    )
    (projected,) = call(
        last_kernel,
        [(rows, 2 * WIDTH)],
        [angles] + [block] * 2,
        [grad2, grad3, near_block, done_block, turns],
        4 * rows * WIDTH * STEPS,
    )
    return eigen, projected


def solution(mesh):
    return jax.shard_map(
        body,
        mesh=mesh,
        in_specs=(P(None, "blk"), P("rep", "blk")),
        out_specs=(P("blk"), P("rep", "blk")),
        check_vma=False,
    )
```

```python
import functools
import jax
import jax.numpy as jnp
from jax import lax
from jax.experimental import pallas as pl
from jax.experimental.pallas import tpu as pltpu
from jax.sharding import PartitionSpec as P

ROOT_ROWS = 256
SWEEPS = 4
WIDTH = 512
LANES = 128
HALO = 16
GROUPS = LANES // HALO
HALO_ROWS = ROOT_ROWS // GROUPS
CHUNK_ROWS = ROOT_ROWS + HALO_ROWS
PARTS = WIDTH // LANES
ROUND_PAIRS = (((0, 0), (1, 1), (2, 2)), ((0, 1), (1, 2)), ((0, 2),))
STEPS = SWEEPS * sum(len(pairs) for pairs in ROUND_PAIRS)
EIGEN_ROW = 2 * STEPS
ANGLE_ROWS = 2 * STEPS + 8
MEGA = 1 << 20


def turn_of(tt, bb, tb):
    y = 2.0 * tb
    x = tt - bb
    ax = jnp.abs(x)
    ay = jnp.abs(y)
    top = jnp.maximum(ax, ay)
    none = top == 0.0
    scale = 1.0 / jnp.where(none, 1.0, top)
    xs = jnp.where(none, 1.0, ax * scale)
    ys = jnp.where(none, 0.0, ay * scale)
    squares = xs * xs + ys * ys
    inv = lax.rsqrt(squares)
    big = jnp.sqrt(0.5 + 0.5 * (xs * inv))
    small = 0.5 * (ys * inv) / big
    forward = x >= 0.0
    cosine = jnp.where(forward, big, small)
    size = jnp.where(forward, small, big)
    larger = 0.5 * (tt + bb) + 0.5 * (top * (squares * inv))
    return cosine, jnp.where(y < 0.0, -size, size), larger


def total8(acc):
    return jnp.sum(acc, axis=0, keepdims=True)


def added(acc, *new):
    return list(new) if acc is None else [x + y for x, y in zip(acc, new)]


def wide8(row):
    return jnp.broadcast_to(row, (8, LANES))


def even_slot():
    return lax.axis_index("blk") % 2 == 0


def first_kernel(root_ref, back_out, both_out, ahead_out, turn_out, top, bottom, rolled, window):
    tiles = [pl.ds(8 * i, 8) for i in range(ROOT_ROWS // 8)]
    cols = [pl.ds(g * LANES, LANES) for g in range(PARTS)]
    low_cols = [pl.ds(WIDTH + g * LANES, LANES) for g in range(PARTS)]
    last = lax.broadcasted_iota(jnp.int32, (8, LANES), 1) == LANES - 1
    tt, bb, tb = ([None] * PARTS for _ in range(3))
    for g in range(PARTS):
        acc = None
        for rows in tiles:
            t, b = root_ref[rows, cols[g]], root_ref[rows, low_cols[g]]
            acc = added(acc, b * b, t * b, t * t)
        bb[g], tb[g], tt[g] = (total8(x) for x in acc)

    def rotate(step, g):
        cosine, sine, tt[g] = turn_of(tt[g], bb[g], tb[g])
        turn_out[pl.ds(step, 1), cols[g]] = cosine
        turn_out[pl.ds(SWEEPS + step, 1), cols[g]] = sine
        c, s = wide8(cosine), wide8(sine)
        for rows in tiles:
            if step == 0:
                t, b = root_ref[rows, cols[g]], root_ref[rows, low_cols[g]]
            else:
                t, b = top[rows, cols[g]], bottom[rows, cols[g]]
            top[rows, cols[g]] = c * t + s * b
            rolled[rows, cols[g]] = pltpu.roll(c * b - s * t, LANES - 1, 1)

    def shift(step, g):
        acc = None
        for rows in tiles:
            b = jnp.where(last, rolled[rows, cols[(g + 1) % PARTS]], rolled[rows, cols[g]])
            bottom[rows, cols[g]] = b
            acc = added(acc, b * b, top[rows, cols[g]] * b)
        bb[g], tb[g] = (total8(x) for x in acc)

    for step in range(SWEEPS - 1):
        rotate(step, 0)
        for g in range(1, PARTS):
            rotate(step, g)
            shift(step, g - 1)
        shift(step, PARTS - 1)
    for g in range(PARTS):
        cosine, sine, _ = turn_of(tt[g], bb[g], tb[g])
        turn_out[pl.ds(SWEEPS - 1, 1), cols[g]] = cosine
        turn_out[pl.ds(2 * SWEEPS - 1, 1), cols[g]] = sine

    part = lax.axis_index("rep") // PARTS
    here = pl.ds(pl.multiple_of(part * LANES, LANES), LANES)
    after = pl.ds(pl.multiple_of(lax.rem(part + 1, PARTS) * LANES, LANES), LANES)
    lane_group = lax.broadcasted_iota(jnp.int32, (8, LANES), 1) // HALO

    own, behind = pl.ds(0, LANES), pl.ds(LANES, LANES)
    for source, target in ((here, own), (after, behind)):
        c = wide8(turn_out[pl.ds(SWEEPS - 1, 1), source])
        s = wide8(turn_out[pl.ds(2 * SWEEPS - 1, 1), source])
        for rows in tiles:
            t, b = top[rows, source], bottom[rows, source]
            window[rows, target] = c * t + s * b
            rolled[rows, target] = pltpu.roll(c * b - s * t, LANES - 1, 1)

    def folded(block, q):
        out = block[pl.ds(8 * q, 8), behind]
        for g in range(1, GROUPS):
            piece = block[pl.ds(g * HALO_ROWS + 8 * q, 8), behind]
            out = jnp.where(lane_group == g, pltpu.roll(piece, g * HALO, 1), out)
        return out

    even = even_slot()
    for v in range(CHUNK_ROWS // 8):
        if v < ROOT_ROWS // 8:
            rows = pl.ds(8 * v, 8)
            t, b = window[rows, own], jnp.where(last, rolled[rows, behind], rolled[rows, own])
        else:
            t, b = (folded(block, v - ROOT_ROWS // 8) for block in (window, rolled))
        both_out[pl.ds(8 * v, 8), :] = t
        both_out[pl.ds(CHUNK_ROWS + 8 * v, 8), :] = b
        back_out[pl.ds(8 * v, 8), :] = jnp.where(even, b, t)
        ahead_out[pl.ds(8 * v, 8), :] = jnp.where(even, t, b)


def gradient_first_kernel(grad_ref, turn_ref, back_out, both_out, ahead_out):
    even = even_slot()
    rows_all = grad_ref.shape[0]
    tiles = [pl.ds(8 * i, 8) for i in range(rows_all // 8)]
    for step in range(SWEEPS):
        c = jnp.broadcast_to(turn_ref[pl.ds(step, 1), :], (8, WIDTH))
        s = jnp.broadcast_to(turn_ref[pl.ds(SWEEPS + step, 1), :], (8, WIDTH))
        for i, rows in enumerate(tiles):
            low = pl.ds(rows_all + 8 * i, 8)
            if step == 0:
                if i % 2 == 0:
                    pair = grad_ref[pl.ds(8 * i, 16), :].astype(jnp.float32)
                half = pair[:8] if i % 2 == 0 else pair[8:]
                t, b = half[:, :WIDTH], half[:, WIDTH:]
            else:
                t, b = both_out[rows, :], both_out[low, :]
            t, b = c * t + s * b, c * b - s * t
            b = pltpu.roll(b, WIDTH - 1, 1)
            both_out[rows, :] = t
            both_out[low, :] = b
            if step == SWEEPS - 1:
                back_out[rows, :] = jnp.where(even, b, t)
                ahead_out[rows, :] = jnp.where(even, t, b)


def cone_kernel(back, pair_out, pair_in, ahead, turn_out, blocks):
    count = ROOT_ROWS // 8
    per_group = HALO_ROWS // 8
    lane = lax.broadcasted_iota(jnp.int32, (8, LANES), 1)
    lane_group = lane // HALO
    even = even_slot()
    homes = (
        (back, ahead, 0),
        (pair_out, pair_in, 0),
        (pair_in, pair_out, 0),
        (pair_out, pair_in, CHUNK_ROWS),
        (pair_in, pair_out, CHUNK_ROWS),
        (ahead, back, 0),
    )

    def home(index, row):
        on_even, on_odd, first = homes[index]
        rows = pl.ds(first + row, 8)
        return jnp.where(even, on_even[rows, :], on_odd[rows, :])

    def unfolded(places, i):
        g, q = divmod(i, per_group)
        out = None
        for p, index in enumerate(places):
            piece = home(index, ROOT_ROWS + 8 * q)
            piece = pltpu.roll(piece, (p - g) * HALO % LANES, 1)
            out = piece if out is None else jnp.where(lane_group == p, piece, out)
        return out

    def given(index, i):
        return home(index, 8 * i) if index < 6 else blocks[index, pl.ds(8 * i, 8), :]

    for i in range(count):
        rows = pl.ds(8 * i, 8)
        blocks[6, rows, :] = unfolded((0, 1, 2), i)
        blocks[7, rows, :] = unfolded((3, 4, 5), i)

    def stored(index, i):
        return blocks[index, pl.ds(8 * i, 8), :]

    tt, bb, tb = ({} for _ in range(3))
    for p, (ti, bi) in enumerate(ROUND_PAIRS[0] + ((6, 4),)):
        acc = None
        for i in range(count):
            rows = pl.ds(8 * i, 8)
            t, b = given(ti, i), given(3 + bi, i)
            if p < 3:
                t, b = pltpu.roll(t, p * HALO, 1), pltpu.roll(b, p * HALO, 1)
                blocks[ti, rows, :] = t
                blocks[3 + bi, rows, :] = b
            acc = added(acc, b * b, t * b, t * t)
        bb[p], tb[p], tt[p] = (total8(x) for x in acc)

    steps = SWEEPS * len(ROUND_PAIRS)
    turns = {}

    def angles(n, p):
        if n >= steps:
            return
        cosine, sine, tt[p] = turn_of(tt[p], bb[p], tb[p])
        if p < 3:
            number, k = divmod(n, SWEEPS)
            row = SWEEPS * sum(len(q) for q in ROUND_PAIRS[:number]) + p * SWEEPS + k
            turn_out[0, pl.ds(row, 1), :] = cosine
            turn_out[0, pl.ds(STEPS + row, 1), :] = sine
        turns[p] = wide8(cosine), wide8(sine)

    def shift_of(n):
        return LANES - 1 - (HALO if n % SWEEPS == SWEEPS - 1 and n + 1 < steps else 0)

    def turn_halo(n):
        if n >= steps:
            return
        c, s = turns[3]
        acc = None
        for i in range(count):
            rows = pl.ds(8 * i, 8)
            t, b = stored(6, i), stored(7 + n % 3, i)
            t, b = c * t + s * b, c * b - s * t
            b = pltpu.roll(b, shift_of(n), 1)
            blocks[6, rows, :] = t
            blocks[7 + (n + 1) % 3, rows, :] = b
            acc = added(acc, b * b, t * b)
        bb[3], tb[3] = (total8(x) for x in acc)

    def turn_pair(n, p):
        number, k = divmod(n, SWEEPS)
        pairs = ROUND_PAIRS[number]
        ti, bi = pairs[p]
        ends = k + 1 == SWEEPS
        final = ends and number + 1 == len(ROUND_PAIRS)
        c, s = turns[p]
        need_top = not ends or p + 1 < len(pairs) or final
        need_bottom = not ends or p > 0 or final
        q = p - 1 if ends and not final else p
        by = shift_of(n)
        enters = lane == (q * HALO - 1) % LANES
        acc = None
        for i in range(count):
            rows = pl.ds(8 * i, 8)
            t, b = stored(ti, i), stored(3 + bi, i)
            top = c * t + s * b
            if need_top and not final:
                blocks[ti, rows, :] = top
            if need_bottom:
                entering = stored(7 + (n + 1) % 3, i)
                b = jnp.where(enters, entering, pltpu.roll(c * b - s * t, by, 1))
                if not final:
                    blocks[3 + bi, rows, :] = b
                other = top if q == p else stored(pairs[q][0], i)
                acc = added(acc, b * b, other * b)
        if need_bottom:
            bb[q], tb[q] = (total8(x) for x in acc)

    angles(0, 3)
    turn_halo(0)
    angles(1, 3)
    for n in range(steps):
        n_pairs = len(ROUND_PAIRS[n // SWEEPS])
        angles(n, 0)
        turn_halo(n + 1)
        for p in range(n_pairs):
            if p + 1 < n_pairs:
                angles(n, p + 1)
            if p == n_pairs - 1:
                angles(n + 2, 3)
            turn_pair(n, p)
    base = 0
    for pairs in ROUND_PAIRS:
        for p in range(len(pairs)):
            for first in (base, STEPS + base):
                rows = pl.ds(first + p * SWEEPS, SWEEPS)
                if p:
                    turn_out[0, rows, :] = pltpu.roll(turn_out[0, rows, :], LANES - p * HALO, 1)
        base += len(pairs) * SWEEPS
    turn_out[0, pl.ds(EIGEN_ROW, 1), :] = tt[0] * (1.0 / ROOT_ROWS)
    turn_out[0, pl.ds(EIGEN_ROW + 1, 1), :] = bb[0] * (1.0 / ROOT_ROWS)
    turn_out[0, pl.ds(EIGEN_ROW + 2, 6), :] = jnp.zeros((6, LANES), jnp.float32)
    for copy in range(1, PARTS):
        turn_out[copy] = turn_out[0]


def widened(turns, wide):
    for part in range(PARTS):
        wide[:, pl.ds(part * LANES, LANES)] = turns[part]


def turned_pair(wide, row, source, target, count, finish):
    for k in range(SWEEPS):
        c = jnp.broadcast_to(wide[pl.ds(row + k, 1), :], (8, WIDTH))
        s = jnp.broadcast_to(wide[pl.ds(STEPS + row + k, 1), :], (8, WIDTH))
        for i in range(count):
            rows = pl.ds(8 * i, 8)
            t, b = source(i) if k == 0 else (target[0][rows, :], target[1][rows, :])
            t, b = c * t + s * b, c * b - s * t
            if k + 1 == SWEEPS:
                finish(i, t, b)
            else:
                target[0][rows, :] = t
                target[1][rows, :] = pltpu.roll(b, WIDTH - 1, 1)


def row_of(pair_round, even_pair, odd_pair):
    base = SWEEPS * sum(len(pairs) for pairs in ROUND_PAIRS[:pair_round])
    return jnp.where(even_slot(), base + SWEEPS * even_pair, base + SWEEPS * odd_pair)


def middle_kernel(back, pair_out, pair_in, turns, eigen_out, near_out, done_out, wide, t0, b0, t1, b1):
    rows_all = back.shape[0]
    count = rows_all // 8
    even = even_slot()
    widened(turns, wide)

    def parts(i):
        rows, low = pl.ds(8 * i, 8), pl.ds(rows_all + 8 * i, 8)
        return rows, low

    def outer(i):
        rows, low = parts(i)
        far = back[rows, :]
        return jnp.where(even, far, pair_out[rows, :]), jnp.where(even, pair_out[low, :], far)

    def inner(i):
        rows, low = parts(i)
        return (
            jnp.where(even, pair_out[rows, :], pair_in[rows, :]),
            jnp.where(even, pair_in[low, :], pair_out[low, :]),
        )

    def keep_outer(i, t, b):
        t0[parts(i)[0], :] = jnp.where(even, t, pltpu.roll(b, WIDTH - 1, 1))

    def keep_inner(i, t, b):
        rows = parts(i)[0]
        t1[rows, :] = t
        b1[rows, :] = pltpu.roll(b, WIDTH - 1, 1)
        near_out[rows, :] = jnp.where(even, t, b1[rows, :])

    def second(i):
        rows = parts(i)[0]
        kept = t0[rows, :]
        return jnp.where(even, kept, t1[rows, :]), jnp.where(even, b1[rows, :], kept)

    def keep_second(i, t, b):
        done_out[parts(i)[0], :] = jnp.where(even, t, pltpu.roll(b, WIDTH - 1, 1))

    turned_pair(wide, row_of(0, 0, 2), outer, (t0, b0), count, keep_outer)
    turned_pair(wide, row_of(0, 1, 1), inner, (t1, b1), count, keep_inner)
    turned_pair(wide, row_of(1, 0, 1), second, (t1, b1), count, keep_second)

    eigen_out[pl.ds(0, WIDTH)] = wide[EIGEN_ROW, :]
    bottom = pltpu.roll(wide[pl.ds(EIGEN_ROW + 1, 1), :], 4 * SWEEPS, 1)
    eigen_out[pl.ds(WIDTH, WIDTH)] = bottom[0]


def last_kernel(pair_in, ahead, near, done, turns, projected_out, wide, t0, b0):
    rows_all = ahead.shape[0]
    count = rows_all // 8
    even = even_slot()
    widened(turns, wide)

    def first(i):
        rows, low = pl.ds(8 * i, 8), pl.ds(rows_all + 8 * i, 8)
        far = ahead[rows, :]
        return jnp.where(even, pair_in[rows, :], far), jnp.where(even, far, pair_in[low, :])

    def keep(i, t, b):
        t0[pl.ds(8 * i, 8), :] = jnp.where(even, pltpu.roll(b, WIDTH - 1, 1), t)

    def with_kept(other):
        def source(i):
            rows = pl.ds(8 * i, 8)
            kept, held = t0[rows, :], other[rows, :]
            return jnp.where(even, held, kept), jnp.where(even, kept, held)

        return source

    def write(i, t, b):
        rows = pl.ds(8 * i, 8)
        b = pltpu.roll(b, 4 * SWEEPS - 1, 1)
        projected_out[rows, pl.ds(0, WIDTH)] = t * t
        projected_out[rows, pl.ds(WIDTH, WIDTH)] = b * b

    turned_pair(wide, row_of(0, 2, 0), first, (t0, b0), count, keep)
    turned_pair(wide, row_of(1, 1, 0), with_kept(near), (t0, b0), count, keep)
    turned_pair(wide, row_of(2, 0, 0), with_kept(done), (t0, b0), count, write)


def call(kernel, outs, scratch, args, flops):
    f32 = jnp.float32
    vmem = pl.BlockSpec(memory_space=pltpu.VMEM)
    shapes = tuple(jax.ShapeDtypeStruct(shape, f32) for shape in outs)
    moved = sum(a.size * a.dtype.itemsize for a in args) + sum(4 * s.size for s in shapes)
    return pl.pallas_call(
        kernel,
        out_shape=shapes,
        in_specs=[vmem] * len(args),
        out_specs=tuple(vmem for _ in shapes),
        scratch_shapes=[pltpu.VMEM(shape, f32) for shape in scratch],
        compiler_params=pltpu.CompilerParams(vmem_limit_bytes=24 * MEGA),
        cost_estimate=pl.CostEstimate(flops=flops, bytes_accessed=moved, transcendentals=0),
    )(*args)


def swapped(shard, by):
    length = lax.axis_size("blk")
    return lax.ppermute(
        shard, "blk", [((i + (by if i % 2 == 0 else -by)) % length, i) for i in range(length)]
    )


def body(root_rows, gradient):
    rows = gradient.shape[0]
    back_root, both_root, ahead_root, turn0 = call(
        first_kernel,
        [(CHUNK_ROWS, LANES), (2 * CHUNK_ROWS, LANES), (CHUNK_ROWS, LANES), (2 * SWEEPS, WIDTH)],
        [(ROOT_ROWS, WIDTH)] * 3 + [(ROOT_ROWS, 2 * LANES)],
        [root_rows],
        16 * ROOT_ROWS * WIDTH * SWEEPS,
    )
    root3 = swapped(ahead_root, 3)
    root0 = swapped(back_root, -3)
    root1 = swapped(both_root, -1)
    root2 = swapped(both_root, 1)
    back_grad, both_grad, ahead_grad = call(
        gradient_first_kernel,
        [(rows, WIDTH), (2 * rows, WIDTH), (rows, WIDTH)],
        [],
        [gradient, turn0],
        8 * rows * WIDTH * SWEEPS,
    )
    def after(value, *others):
        return lax.optimization_barrier((value, *others))[0]

    grad1 = swapped(after(both_grad, root0), -1)
    grad2 = swapped(after(both_grad, root3), 1)
    grad0 = swapped(after(back_grad, root1), -3)
    grad3 = swapped(after(ahead_grad, root2), 3)
    (turns,) = call(
        cone_kernel,
        [(PARTS, ANGLE_ROWS, LANES)],
        [(10, ROOT_ROWS, LANES)],
        [root0, root1, root2, root3],
        16 * CHUNK_ROWS * LANES * STEPS,
    )
    reps = lax.axis_size("rep")
    near = reps // PARTS
    groups = [[x * near + z for x in range(PARTS)] for z in range(near)]
    turns = lax.all_to_all(turns, "rep", 0, 0, axis_index_groups=groups)
    block, angles = (rows, WIDTH), (ANGLE_ROWS, WIDTH)
    eigen, near_block, done_block = call(
        middle_kernel,
        [(2 * WIDTH,), block, block],
        [angles] + [block] * 4,
        [grad0, grad1, grad2, turns],
        4 * rows * WIDTH * STEPS,
    )
    (projected,) = call(
        last_kernel,
        [(rows, 2 * WIDTH)],
        [angles] + [block] * 2,
        [grad2, grad3, near_block, done_block, turns],
        4 * rows * WIDTH * STEPS,
    )
    return eigen, projected


def solution(mesh):
    return jax.shard_map(
        body,
        mesh=mesh,
        in_specs=(P(None, "blk"), P("rep", "blk")),
        out_specs=(P("blk"), P("rep", "blk")),
        check_vma=False,
    )
```

```python
import functools
import jax
import jax.numpy as jnp
from jax import lax
from jax.experimental import pallas as pl
from jax.experimental.pallas import tpu as pltpu
from jax.sharding import PartitionSpec as P

ROOT_ROWS = 256
SWEEPS = 4
OUT_COPIES = 4
LAST_PARTS = 1
WIDTH = 512
LANES = 128
HALO = 16
GROUPS = LANES // HALO
HALO_ROWS = ROOT_ROWS // GROUPS
CHUNK_ROWS = ROOT_ROWS + HALO_ROWS
PARTS = WIDTH // LANES
ROUND_PAIRS = (((0, 0), (1, 1), (2, 2)), ((0, 1), (1, 2)), ((0, 2),))
STEPS = SWEEPS * sum(len(pairs) for pairs in ROUND_PAIRS)
EIGEN_ROW = 2 * STEPS
ANGLE_ROWS = 2 * STEPS + 8
MEGA = 1 << 20


def turn_of(tt, bb, tb):
    y = 2.0 * tb
    x = tt - bb
    ax = jnp.abs(x)
    ay = jnp.abs(y)
    top = jnp.maximum(ax, ay)
    none = top == 0.0
    scale = 1.0 / jnp.where(none, 1.0, top)
    xs = jnp.where(none, 1.0, ax * scale)
    ys = jnp.where(none, 0.0, ay * scale)
    squares = xs * xs + ys * ys
    inv = lax.rsqrt(squares)
    big = jnp.sqrt(0.5 + 0.5 * (xs * inv))
    small = 0.5 * (ys * inv) / big
    forward = x >= 0.0
    cosine = jnp.where(forward, big, small)
    size = jnp.where(forward, small, big)
    larger = 0.5 * (tt + bb) + 0.5 * (top * (squares * inv))
    return cosine, jnp.where(y < 0.0, -size, size), larger


def total8(acc):
    return jnp.sum(acc, axis=0, keepdims=True)


def added(acc, *new):
    return list(new) if acc is None else [x + y for x, y in zip(acc, new)]


def wide8(row):
    return jnp.broadcast_to(row, (8, LANES))


def even_slot():
    return lax.axis_index("blk") % 2 == 0


def first_kernel(root_ref, back_out, both_out, ahead_out, turn_out, top, bottom, rolled, window):
    tiles = [pl.ds(8 * i, 8) for i in range(ROOT_ROWS // 8)]
    cols = [pl.ds(g * LANES, LANES) for g in range(PARTS)]
    low_cols = [pl.ds(WIDTH + g * LANES, LANES) for g in range(PARTS)]
    last = lax.broadcasted_iota(jnp.int32, (8, LANES), 1) == LANES - 1
    tt, bb, tb = ([None] * PARTS for _ in range(3))
    for g in range(PARTS):
        acc = None
        for rows in tiles:
            t, b = root_ref[rows, cols[g]], root_ref[rows, low_cols[g]]
            acc = added(acc, b * b, t * b, t * t)
        bb[g], tb[g], tt[g] = (total8(x) for x in acc)

    def rotate(step, g):
        cosine, sine, tt[g] = turn_of(tt[g], bb[g], tb[g])
        turn_out[pl.ds(step, 1), cols[g]] = cosine
        turn_out[pl.ds(SWEEPS + step, 1), cols[g]] = sine
        c, s = wide8(cosine), wide8(sine)
        for rows in tiles:
            if step == 0:
                t, b = root_ref[rows, cols[g]], root_ref[rows, low_cols[g]]
            else:
                t, b = top[rows, cols[g]], bottom[rows, cols[g]]
            top[rows, cols[g]] = c * t + s * b
            rolled[rows, cols[g]] = pltpu.roll(c * b - s * t, LANES - 1, 1)

    def shift(step, g):
        acc = None
        for rows in tiles:
            b = jnp.where(last, rolled[rows, cols[(g + 1) % PARTS]], rolled[rows, cols[g]])
            bottom[rows, cols[g]] = b
            acc = added(acc, b * b, top[rows, cols[g]] * b)
        bb[g], tb[g] = (total8(x) for x in acc)

    for step in range(SWEEPS - 1):
        rotate(step, 0)
        for g in range(1, PARTS):
            rotate(step, g)
            shift(step, g - 1)
        shift(step, PARTS - 1)
    for g in range(PARTS):
        cosine, sine, _ = turn_of(tt[g], bb[g], tb[g])
        turn_out[pl.ds(SWEEPS - 1, 1), cols[g]] = cosine
        turn_out[pl.ds(2 * SWEEPS - 1, 1), cols[g]] = sine

    part = lax.axis_index("rep") // PARTS
    here = pl.ds(pl.multiple_of(part * LANES, LANES), LANES)
    after = pl.ds(pl.multiple_of(lax.rem(part + 1, PARTS) * LANES, LANES), LANES)
    lane_group = lax.broadcasted_iota(jnp.int32, (8, LANES), 1) // HALO

    own, behind = pl.ds(0, LANES), pl.ds(LANES, LANES)
    for source, target in ((here, own), (after, behind)):
        c = wide8(turn_out[pl.ds(SWEEPS - 1, 1), source])
        s = wide8(turn_out[pl.ds(2 * SWEEPS - 1, 1), source])
        for rows in tiles:
            t, b = top[rows, source], bottom[rows, source]
            window[rows, target] = c * t + s * b
            rolled[rows, target] = pltpu.roll(c * b - s * t, LANES - 1, 1)

    def folded(block, q):
        out = block[pl.ds(8 * q, 8), behind]
        for g in range(1, GROUPS):
            piece = block[pl.ds(g * HALO_ROWS + 8 * q, 8), behind]
            out = jnp.where(lane_group == g, pltpu.roll(piece, g * HALO, 1), out)
        return out

    even = even_slot()
    for v in range(CHUNK_ROWS // 8):
        if v < ROOT_ROWS // 8:
            rows = pl.ds(8 * v, 8)
            t, b = window[rows, own], jnp.where(last, rolled[rows, behind], rolled[rows, own])
        else:
            t, b = (folded(block, v - ROOT_ROWS // 8) for block in (window, rolled))
        both_out[pl.ds(8 * v, 8), :] = t
        both_out[pl.ds(CHUNK_ROWS + 8 * v, 8), :] = b
        back_out[pl.ds(8 * v, 8), :] = jnp.where(even, b, t)
        ahead_out[pl.ds(8 * v, 8), :] = jnp.where(even, t, b)


def gradient_first_kernel(grad_ref, turn_ref, back_out, both_out, ahead_out):
    even = even_slot()
    rows_all = grad_ref.shape[0]
    tiles = [pl.ds(8 * i, 8) for i in range(rows_all // 8)]
    for step in range(SWEEPS):
        c = jnp.broadcast_to(turn_ref[pl.ds(step, 1), :], (8, WIDTH))
        s = jnp.broadcast_to(turn_ref[pl.ds(SWEEPS + step, 1), :], (8, WIDTH))
        for i, rows in enumerate(tiles):
            low = pl.ds(rows_all + 8 * i, 8)
            if step == 0:
                if i % 2 == 0:
                    pair = grad_ref[pl.ds(8 * i, 16), :].astype(jnp.float32)
                half = pair[:8] if i % 2 == 0 else pair[8:]
                t, b = half[:, :WIDTH], half[:, WIDTH:]
            else:
                t, b = both_out[rows, :], both_out[low, :]
            t, b = c * t + s * b, c * b - s * t
            b = pltpu.roll(b, WIDTH - 1, 1)
            both_out[rows, :] = t
            both_out[low, :] = b
            if step == SWEEPS - 1:
                back_out[rows, :] = jnp.where(even, b, t)
                ahead_out[rows, :] = jnp.where(even, t, b)


def cone_kernel(back, pair_out, pair_in, ahead, turn_out, blocks):
    count = ROOT_ROWS // 8
    per_group = HALO_ROWS // 8
    lane = lax.broadcasted_iota(jnp.int32, (8, LANES), 1)
    lane_group = lane // HALO
    even = even_slot()
    homes = (
        (back, ahead, 0),
        (pair_out, pair_in, 0),
        (pair_in, pair_out, 0),
        (pair_out, pair_in, CHUNK_ROWS),
        (pair_in, pair_out, CHUNK_ROWS),
        (ahead, back, 0),
    )

    def home(index, row):
        on_even, on_odd, first = homes[index]
        rows = pl.ds(first + row, 8)
        return jnp.where(even, on_even[rows, :], on_odd[rows, :])

    def unfolded(places, i):
        g, q = divmod(i, per_group)
        out = None
        for p, index in enumerate(places):
            piece = home(index, ROOT_ROWS + 8 * q)
            piece = pltpu.roll(piece, (p - g) * HALO % LANES, 1)
            out = piece if out is None else jnp.where(lane_group == p, piece, out)
        return out

    def given(index, i):
        return home(index, 8 * i) if index < 6 else blocks[index, pl.ds(8 * i, 8), :]

    for i in range(count):
        rows = pl.ds(8 * i, 8)
        blocks[6, rows, :] = unfolded((0, 1, 2), i)
        blocks[7, rows, :] = unfolded((3, 4, 5), i)

    def stored(index, i):
        return blocks[index, pl.ds(8 * i, 8), :]

    tt, bb, tb = ({} for _ in range(3))
    for p, (ti, bi) in enumerate(ROUND_PAIRS[0] + ((6, 4),)):
        acc = None
        for i in range(count):
            rows = pl.ds(8 * i, 8)
            t, b = given(ti, i), given(3 + bi, i)
            if p < 3:
                t, b = pltpu.roll(t, p * HALO, 1), pltpu.roll(b, p * HALO, 1)
                blocks[ti, rows, :] = t
                blocks[3 + bi, rows, :] = b
            acc = added(acc, b * b, t * b, t * t)
        bb[p], tb[p], tt[p] = (total8(x) for x in acc)

    steps = SWEEPS * len(ROUND_PAIRS)
    turns = {}

    def angles(n, p):
        if n >= steps:
            return
        cosine, sine, tt[p] = turn_of(tt[p], bb[p], tb[p])
        if p < 3:
            number, k = divmod(n, SWEEPS)
            row = SWEEPS * sum(len(q) for q in ROUND_PAIRS[:number]) + p * SWEEPS + k
            turn_out[0, pl.ds(row, 1), :] = cosine
            turn_out[0, pl.ds(STEPS + row, 1), :] = sine
        turns[p] = wide8(cosine), wide8(sine)

    def shift_of(n):
        return LANES - 1 - (HALO if n % SWEEPS == SWEEPS - 1 and n + 1 < steps else 0)

    def turn_halo(n):
        if n >= steps:
            return
        c, s = turns[3]
        acc = None
        for i in range(count):
            rows = pl.ds(8 * i, 8)
            t, b = stored(6, i), stored(7 + n % 3, i)
            t, b = c * t + s * b, c * b - s * t
            b = pltpu.roll(b, shift_of(n), 1)
            blocks[6, rows, :] = t
            blocks[7 + (n + 1) % 3, rows, :] = b
            acc = added(acc, b * b, t * b)
        bb[3], tb[3] = (total8(x) for x in acc)

    def turn_pair(n, p):
        number, k = divmod(n, SWEEPS)
        pairs = ROUND_PAIRS[number]
        ti, bi = pairs[p]
        ends = k + 1 == SWEEPS
        final = ends and number + 1 == len(ROUND_PAIRS)
        c, s = turns[p]
        need_top = not ends or p + 1 < len(pairs) or final
        need_bottom = not ends or p > 0 or final
        q = p - 1 if ends and not final else p
        by = shift_of(n)
        enters = lane == (q * HALO - 1) % LANES
        acc = None
        for i in range(count):
            rows = pl.ds(8 * i, 8)
            t, b = stored(ti, i), stored(3 + bi, i)
            top = c * t + s * b
            if need_top and not final:
                blocks[ti, rows, :] = top
            if need_bottom:
                entering = stored(7 + (n + 1) % 3, i)
                b = jnp.where(enters, entering, pltpu.roll(c * b - s * t, by, 1))
                if not final:
                    blocks[3 + bi, rows, :] = b
                other = top if q == p else stored(pairs[q][0], i)
                acc = added(acc, b * b, other * b)
        if need_bottom:
            bb[q], tb[q] = (total8(x) for x in acc)

    angles(0, 3)
    turn_halo(0)
    angles(1, 3)
    for n in range(steps):
        n_pairs = len(ROUND_PAIRS[n // SWEEPS])
        angles(n, 0)
        turn_halo(n + 1)
        for p in range(n_pairs):
            if p + 1 < n_pairs:
                angles(n, p + 1)
            if p == n_pairs - 1:
                angles(n + 2, 3)
            turn_pair(n, p)
    base = 0
    for pairs in ROUND_PAIRS:
        for p in range(len(pairs)):
            for first in (base, STEPS + base):
                rows = pl.ds(first + p * SWEEPS, SWEEPS)
                if p:
                    turn_out[0, rows, :] = pltpu.roll(turn_out[0, rows, :], LANES - p * HALO, 1)
        base += len(pairs) * SWEEPS
    turn_out[0, pl.ds(EIGEN_ROW, 1), :] = tt[0] * (1.0 / ROOT_ROWS)
    turn_out[0, pl.ds(EIGEN_ROW + 1, 1), :] = bb[0] * (1.0 / ROOT_ROWS)
    turn_out[0, pl.ds(EIGEN_ROW + 2, 6), :] = jnp.zeros((6, LANES), jnp.float32)
    for copy in range(1, PARTS):
        turn_out[copy] = turn_out[0]


def widened(turns, wide):
    for part in range(PARTS):
        wide[:, pl.ds(part * LANES, LANES)] = turns[part]


def turned_pair(wide, row, source, target, tiles, finish):
    for k in range(SWEEPS):
        c = jnp.broadcast_to(wide[pl.ds(row + k, 1), :], (8, WIDTH))
        s = jnp.broadcast_to(wide[pl.ds(STEPS + row + k, 1), :], (8, WIDTH))
        for i in tiles:
            rows = pl.ds(8 * i, 8)
            t, b = source(i) if k == 0 else (target[0][rows, :], target[1][rows, :])
            t, b = c * t + s * b, c * b - s * t
            if k + 1 == SWEEPS:
                finish(i, t, b)
            else:
                target[0][rows, :] = t
                target[1][rows, :] = pltpu.roll(b, WIDTH - 1, 1)


def row_of(pair_round, even_pair, odd_pair):
    base = SWEEPS * sum(len(pairs) for pairs in ROUND_PAIRS[:pair_round])
    return jnp.where(even_slot(), base + SWEEPS * even_pair, base + SWEEPS * odd_pair)


def middle_kernel(back, pair_out, pair_in, turns, eigen_out, near_out, done_out, wide, t0, b0, t1, b1):
    rows_all = back.shape[0]
    count = rows_all // 8
    even = even_slot()
    widened(turns, wide)

    def parts(i):
        rows, low = pl.ds(8 * i, 8), pl.ds(rows_all + 8 * i, 8)
        return rows, low

    def outer(i):
        rows, low = parts(i)
        far = back[rows, :]
        return jnp.where(even, far, pair_out[rows, :]), jnp.where(even, pair_out[low, :], far)

    def inner(i):
        rows, low = parts(i)
        return (
            jnp.where(even, pair_out[rows, :], pair_in[rows, :]),
            jnp.where(even, pair_in[low, :], pair_out[low, :]),
        )

    def keep_outer(i, t, b):
        t0[parts(i)[0], :] = jnp.where(even, t, pltpu.roll(b, WIDTH - 1, 1))

    def keep_inner(i, t, b):
        rows = parts(i)[0]
        t1[rows, :] = t
        b1[rows, :] = pltpu.roll(b, WIDTH - 1, 1)
        near_out[rows, :] = jnp.where(even, t, b1[rows, :])

    def second(i):
        rows = parts(i)[0]
        kept = t0[rows, :]
        return jnp.where(even, kept, t1[rows, :]), jnp.where(even, b1[rows, :], kept)

    def keep_second(i, t, b):
        done_out[parts(i)[0], :] = jnp.where(even, t, pltpu.roll(b, WIDTH - 1, 1))

    turned_pair(wide, row_of(0, 0, 2), outer, (t0, b0), range(count), keep_outer)
    turned_pair(wide, row_of(0, 1, 1), inner, (t1, b1), range(count), keep_inner)
    turned_pair(wide, row_of(1, 0, 1), second, (t1, b1), range(count), keep_second)

    eigen_out[pl.ds(0, WIDTH)] = wide[EIGEN_ROW, :]
    bottom = pltpu.roll(wide[pl.ds(EIGEN_ROW + 1, 1), :], 4 * SWEEPS, 1)
    eigen_out[pl.ds(WIDTH, WIDTH)] = bottom[0]


def last_kernel(pair_in, ahead, near, done, wide, projected_out, t0, b0, result, left):
    rows_all = ahead.shape[0]
    count = rows_all // 8
    even = even_slot()

    def first(i):
        rows, low = pl.ds(8 * i, 8), pl.ds(rows_all + 8 * i, 8)
        far = ahead[rows, :]
        return jnp.where(even, pair_in[rows, :], far), jnp.where(even, far, pair_in[low, :])

    def keep(i, t, b):
        t0[pl.ds(8 * i, 8), :] = jnp.where(even, pltpu.roll(b, WIDTH - 1, 1), t)

    def with_kept(other):
        def source(i):
            rows = pl.ds(8 * i, 8)
            kept, held = t0[rows, :], other[rows, :]
            return jnp.where(even, held, kept), jnp.where(even, kept, held)

        return source

    def write(i, t, b):
        rows = pl.ds(8 * i, 8)
        b = pltpu.roll(b, 4 * SWEEPS - 1, 1)
        result[rows, pl.ds(0, WIDTH)] = t * t
        result[rows, pl.ds(WIDTH, WIDTH)] = b * b
        if (i + 1) % per_copy == 0:
            copies[i // per_copy].start()

    per_copy = count // OUT_COPIES
    size = 8 * per_copy
    copies = [
        pltpu.make_async_copy(
            result.at[pl.ds(j * size, size), :], projected_out.at[pl.ds(j * size, size), :], left.at[j]
        )
        for j in range(OUT_COPIES)
    ]
    turned_pair(wide, row_of(0, 2, 0), first, (t0, b0), range(count), keep)
    turned_pair(wide, row_of(1, 1, 0), with_kept(near), (t0, b0), range(count), keep)
    each = count // LAST_PARTS
    for first_tile in range(0, count, each):
        tiles = range(first_tile, first_tile + each)
        turned_pair(wide, row_of(2, 0, 0), with_kept(done), (t0, b0), tiles, write)
    for copy in copies:
        copy.wait()


def call(kernel, outs, scratch, args, flops, copies=0):
    f32 = jnp.float32
    vmem = pl.BlockSpec(memory_space=pltpu.VMEM)
    shapes = tuple(jax.ShapeDtypeStruct(shape, f32) for shape in outs)
    moved = sum(a.size * a.dtype.itemsize for a in args) + sum(4 * s.size for s in shapes)
    return pl.pallas_call(
        kernel,
        out_shape=shapes,
        in_specs=[vmem] * len(args),
        out_specs=tuple(pl.BlockSpec(memory_space=pl.ANY) if copies else vmem for _ in shapes),
        scratch_shapes=[pltpu.VMEM(shape, f32) for shape in scratch]
        + ([pltpu.SemaphoreType.DMA((copies,))] if copies else []),
        compiler_params=pltpu.CompilerParams(vmem_limit_bytes=24 * MEGA),
        cost_estimate=pl.CostEstimate(flops=flops, bytes_accessed=moved, transcendentals=0),
    )(*args)


def swapped(shard, by):
    length = lax.axis_size("blk")
    return lax.ppermute(
        shard, "blk", [((i + (by if i % 2 == 0 else -by)) % length, i) for i in range(length)]
    )


def body(root_rows, gradient):
    rows = gradient.shape[0]
    back_root, both_root, ahead_root, turn0 = call(
        first_kernel,
        [(CHUNK_ROWS, LANES), (2 * CHUNK_ROWS, LANES), (CHUNK_ROWS, LANES), (2 * SWEEPS, WIDTH)],
        [(ROOT_ROWS, WIDTH)] * 3 + [(ROOT_ROWS, 2 * LANES)],
        [root_rows],
        16 * ROOT_ROWS * WIDTH * SWEEPS,
    )
    root3 = swapped(ahead_root, 3)
    root0 = swapped(back_root, -3)
    root1 = swapped(both_root, -1)
    root2 = swapped(both_root, 1)
    back_grad, both_grad, ahead_grad = call(
        gradient_first_kernel,
        [(rows, WIDTH), (2 * rows, WIDTH), (rows, WIDTH)],
        [],
        [gradient, turn0],
        8 * rows * WIDTH * SWEEPS,
    )
    def after(value, *others):
        return lax.optimization_barrier((value, *others))[0]

    grad1 = swapped(after(both_grad, root0), -1)
    grad2 = swapped(after(both_grad, root3), 1)
    grad0 = swapped(after(back_grad, root1), -3)
    grad3 = swapped(after(ahead_grad, root2), 3)
    (turns,) = call(
        cone_kernel,
        [(PARTS, ANGLE_ROWS, LANES)],
        [(10, ROOT_ROWS, LANES)],
        [root0, root1, root2, root3],
        16 * CHUNK_ROWS * LANES * STEPS,
    )
    reps = lax.axis_size("rep")
    near = reps // PARTS
    groups = [[x * near + z for x in range(PARTS)] for z in range(near)]
    turns = lax.all_to_all(turns, "rep", 0, 0, axis_index_groups=groups)
    block, angles = (rows, WIDTH), (ANGLE_ROWS, WIDTH)
    eigen, near_block, done_block, wide_turns = call(
        middle_kernel,
        [(2 * WIDTH,), block, block, angles],
        [block] * 4,
        [grad0, grad1, grad2, turns],
        4 * rows * WIDTH * STEPS,
    )
    (projected,) = call(
        last_kernel,
        [(rows, 2 * WIDTH)],
        [block] * 2 + [(rows, 2 * WIDTH)],
        [grad2, grad3, near_block, done_block, wide_turns],
        4 * rows * WIDTH * STEPS,
        copies=OUT_COPIES,
    )
    return eigen, projected


def solution(mesh):
    return jax.shard_map(
        body,
        mesh=mesh,
        in_specs=(P(None, "blk"), P("rep", "blk")),
        out_specs=(P("blk"), P("rep", "blk")),
        check_vma=False,
    )
```

```python
import functools
import jax
import jax.numpy as jnp
from jax import lax
from jax.experimental import pallas as pl
from jax.experimental.pallas import tpu as pltpu
from jax.sharding import PartitionSpec as P

ROOT_ROWS = 256
SWEEPS = 4
WIDTH = 512
LANES = 128
HALO = 16
GROUPS = LANES // HALO
HALO_ROWS = ROOT_ROWS // GROUPS
CHUNK_ROWS = ROOT_ROWS + HALO_ROWS
PARTS = WIDTH // LANES
ROUND_PAIRS = (((0, 0), (1, 1), (2, 2)), ((0, 1), (1, 2)), ((0, 2),))
STEPS = SWEEPS * sum(len(pairs) for pairs in ROUND_PAIRS)
EIGEN_ROW = 2 * STEPS
ANGLE_ROWS = 2 * STEPS + 8
MEGA = 1 << 20


def turn_of(tt, bb, tb):
    y = 2.0 * tb
    x = tt - bb
    ax = jnp.abs(x)
    ay = jnp.abs(y)
    top = jnp.maximum(ax, ay)
    none = top == 0.0
    scale = 1.0 / jnp.where(none, 1.0, top)
    xs = jnp.where(none, 1.0, ax * scale)
    ys = jnp.where(none, 0.0, ay * scale)
    squares = xs * xs + ys * ys
    inv = lax.rsqrt(squares)
    big = jnp.sqrt(0.5 + 0.5 * (xs * inv))
    small = 0.5 * (ys * inv) / big
    forward = x >= 0.0
    cosine = jnp.where(forward, big, small)
    size = jnp.where(forward, small, big)
    larger = 0.5 * (tt + bb) + 0.5 * (top * (squares * inv))
    return cosine, jnp.where(y < 0.0, -size, size), larger


def total8(acc):
    return jnp.sum(acc, axis=0, keepdims=True)


def added(acc, *new):
    return list(new) if acc is None else [x + y for x, y in zip(acc, new)]


def wide8(row):
    return jnp.broadcast_to(row, (8, LANES))


def even_slot():
    return lax.axis_index("blk") % 2 == 0


def first_kernel(root_ref, back_out, both_out, ahead_out, turn_out, top, bottom, rolled, window):
    tiles = [pl.ds(8 * i, 8) for i in range(ROOT_ROWS // 8)]
    cols = [pl.ds(g * LANES, LANES) for g in range(PARTS)]
    low_cols = [pl.ds(WIDTH + g * LANES, LANES) for g in range(PARTS)]
    last = lax.broadcasted_iota(jnp.int32, (8, LANES), 1) == LANES - 1
    tt, bb, tb = ([None] * PARTS for _ in range(3))
    for g in range(PARTS):
        acc = None
        for rows in tiles:
            t, b = root_ref[rows, cols[g]], root_ref[rows, low_cols[g]]
            acc = added(acc, b * b, t * b, t * t)
        bb[g], tb[g], tt[g] = (total8(x) for x in acc)

    def rotate(step, g):
        cosine, sine, tt[g] = turn_of(tt[g], bb[g], tb[g])
        turn_out[pl.ds(step, 1), cols[g]] = cosine
        turn_out[pl.ds(SWEEPS + step, 1), cols[g]] = sine
        c, s = wide8(cosine), wide8(sine)
        for rows in tiles:
            if step == 0:
                t, b = root_ref[rows, cols[g]], root_ref[rows, low_cols[g]]
            else:
                t, b = top[rows, cols[g]], bottom[rows, cols[g]]
            top[rows, cols[g]] = c * t + s * b
            rolled[rows, cols[g]] = pltpu.roll(c * b - s * t, LANES - 1, 1)

    def shift(step, g):
        acc = None
        for rows in tiles:
            b = jnp.where(last, rolled[rows, cols[(g + 1) % PARTS]], rolled[rows, cols[g]])
            bottom[rows, cols[g]] = b
            acc = added(acc, b * b, top[rows, cols[g]] * b)
        bb[g], tb[g] = (total8(x) for x in acc)

    for step in range(SWEEPS - 1):
        rotate(step, 0)
        for g in range(1, PARTS):
            rotate(step, g)
            shift(step, g - 1)
        shift(step, PARTS - 1)
    for g in range(PARTS):
        cosine, sine, _ = turn_of(tt[g], bb[g], tb[g])
        turn_out[pl.ds(SWEEPS - 1, 1), cols[g]] = cosine
        turn_out[pl.ds(2 * SWEEPS - 1, 1), cols[g]] = sine

    part = lax.axis_index("rep") // PARTS
    here = pl.ds(pl.multiple_of(part * LANES, LANES), LANES)
    after = pl.ds(pl.multiple_of(lax.rem(part + 1, PARTS) * LANES, LANES), LANES)
    lane_group = lax.broadcasted_iota(jnp.int32, (8, LANES), 1) // HALO

    own, behind = pl.ds(0, LANES), pl.ds(LANES, LANES)
    for source, target in ((here, own), (after, behind)):
        c = wide8(turn_out[pl.ds(SWEEPS - 1, 1), source])
        s = wide8(turn_out[pl.ds(2 * SWEEPS - 1, 1), source])
        for rows in tiles:
            t, b = top[rows, source], bottom[rows, source]
            window[rows, target] = c * t + s * b
            rolled[rows, target] = pltpu.roll(c * b - s * t, LANES - 1, 1)

    def folded(block, q):
        out = block[pl.ds(8 * q, 8), behind]
        for g in range(1, GROUPS):
            piece = block[pl.ds(g * HALO_ROWS + 8 * q, 8), behind]
            out = jnp.where(lane_group == g, pltpu.roll(piece, g * HALO, 1), out)
        return out

    even = even_slot()
    for v in range(CHUNK_ROWS // 8):
        if v < ROOT_ROWS // 8:
            rows = pl.ds(8 * v, 8)
            t, b = window[rows, own], jnp.where(last, rolled[rows, behind], rolled[rows, own])
        else:
            t, b = (folded(block, v - ROOT_ROWS // 8) for block in (window, rolled))
        both_out[pl.ds(8 * v, 8), :] = t
        both_out[pl.ds(CHUNK_ROWS + 8 * v, 8), :] = b
        back_out[pl.ds(8 * v, 8), :] = jnp.where(even, b, t)
        ahead_out[pl.ds(8 * v, 8), :] = jnp.where(even, t, b)


def gradient_first_kernel(grad_ref, turn_ref, back_out, both_out, ahead_out):
    even = even_slot()
    rows_all = grad_ref.shape[0]
    tiles = [pl.ds(8 * i, 8) for i in range(rows_all // 8)]
    for step in range(SWEEPS):
        c = jnp.broadcast_to(turn_ref[pl.ds(step, 1), :], (8, WIDTH))
        s = jnp.broadcast_to(turn_ref[pl.ds(SWEEPS + step, 1), :], (8, WIDTH))
        for i, rows in enumerate(tiles):
            low = pl.ds(rows_all + 8 * i, 8)
            if step == 0:
                if i % 2 == 0:
                    pair = grad_ref[pl.ds(8 * i, 16), :].astype(jnp.float32)
                half = pair[:8] if i % 2 == 0 else pair[8:]
                t, b = half[:, :WIDTH], half[:, WIDTH:]
            else:
                t, b = both_out[rows, :], both_out[low, :]
            t, b = c * t + s * b, c * b - s * t
            b = pltpu.roll(b, WIDTH - 1, 1)
            both_out[rows, :] = t
            both_out[low, :] = b
            if step == SWEEPS - 1:
                back_out[rows, :] = jnp.where(even, b, t)
                ahead_out[rows, :] = jnp.where(even, t, b)


def cone_kernel(back, pair_out, pair_in, ahead, turn_out, blocks):
    count = ROOT_ROWS // 8
    per_group = HALO_ROWS // 8
    lane = lax.broadcasted_iota(jnp.int32, (8, LANES), 1)
    lane_group = lane // HALO
    even = even_slot()
    homes = (
        (back, ahead, 0),
        (pair_out, pair_in, 0),
        (pair_in, pair_out, 0),
        (pair_out, pair_in, CHUNK_ROWS),
        (pair_in, pair_out, CHUNK_ROWS),
        (ahead, back, 0),
    )

    def home(index, row):
        on_even, on_odd, first = homes[index]
        rows = pl.ds(first + row, 8)
        return jnp.where(even, on_even[rows, :], on_odd[rows, :])

    def unfolded(places, i):
        g, q = divmod(i, per_group)
        out = None
        for p, index in enumerate(places):
            piece = home(index, ROOT_ROWS + 8 * q)
            piece = pltpu.roll(piece, (p - g) * HALO % LANES, 1)
            out = piece if out is None else jnp.where(lane_group == p, piece, out)
        return out

    def given(index, i):
        return home(index, 8 * i) if index < 6 else blocks[index, pl.ds(8 * i, 8), :]

    for i in range(count):
        rows = pl.ds(8 * i, 8)
        blocks[6, rows, :] = unfolded((0, 1, 2), i)
        blocks[7, rows, :] = unfolded((3, 4, 5), i)

    def stored(index, i):
        return blocks[index, pl.ds(8 * i, 8), :]

    tt, bb, tb = ({} for _ in range(3))
    for p, (ti, bi) in enumerate(ROUND_PAIRS[0] + ((6, 4),)):
        acc = None
        for i in range(count):
            rows = pl.ds(8 * i, 8)
            t, b = given(ti, i), given(3 + bi, i)
            if p < 3:
                t, b = pltpu.roll(t, p * HALO, 1), pltpu.roll(b, p * HALO, 1)
                blocks[ti, rows, :] = t
                blocks[3 + bi, rows, :] = b
            acc = added(acc, b * b, t * b, t * t)
        bb[p], tb[p], tt[p] = (total8(x) for x in acc)

    steps = SWEEPS * len(ROUND_PAIRS)
    turns = {}

    def angles(n, p):
        if n >= steps:
            return
        cosine, sine, tt[p] = turn_of(tt[p], bb[p], tb[p])
        if p < 3:
            number, k = divmod(n, SWEEPS)
            row = SWEEPS * sum(len(q) for q in ROUND_PAIRS[:number]) + p * SWEEPS + k
            turn_out[0, pl.ds(row, 1), :] = cosine
            turn_out[0, pl.ds(STEPS + row, 1), :] = sine
        turns[p] = wide8(cosine), wide8(sine)

    def shift_of(n):
        return LANES - 1 - (HALO if n % SWEEPS == SWEEPS - 1 and n + 1 < steps else 0)

    def turn_halo(n):
        if n >= steps:
            return
        c, s = turns[3]
        acc = None
        for i in range(count):
            rows = pl.ds(8 * i, 8)
            t, b = stored(6, i), stored(7 + n % 3, i)
            t, b = c * t + s * b, c * b - s * t
            b = pltpu.roll(b, shift_of(n), 1)
            blocks[6, rows, :] = t
            blocks[7 + (n + 1) % 3, rows, :] = b
            acc = added(acc, b * b, t * b)
        bb[3], tb[3] = (total8(x) for x in acc)

    def turn_pair(n, p):
        number, k = divmod(n, SWEEPS)
        pairs = ROUND_PAIRS[number]
        ti, bi = pairs[p]
        ends = k + 1 == SWEEPS
        final = ends and number + 1 == len(ROUND_PAIRS)
        c, s = turns[p]
        need_top = not ends or p + 1 < len(pairs) or final
        need_bottom = not ends or p > 0 or final
        q = p - 1 if ends and not final else p
        by = shift_of(n)
        enters = lane == (q * HALO - 1) % LANES
        acc = None
        for i in range(count):
            rows = pl.ds(8 * i, 8)
            t, b = stored(ti, i), stored(3 + bi, i)
            top = c * t + s * b
            if need_top and not final:
                blocks[ti, rows, :] = top
            if need_bottom:
                entering = stored(7 + (n + 1) % 3, i)
                b = jnp.where(enters, entering, pltpu.roll(c * b - s * t, by, 1))
                if not final:
                    blocks[3 + bi, rows, :] = b
                other = top if q == p else stored(pairs[q][0], i)
                acc = added(acc, b * b, other * b)
        if need_bottom:
            bb[q], tb[q] = (total8(x) for x in acc)

    angles(0, 3)
    turn_halo(0)
    angles(1, 3)
    for n in range(steps):
        n_pairs = len(ROUND_PAIRS[n // SWEEPS])
        angles(n, 0)
        turn_halo(n + 1)
        for p in range(n_pairs):
            if p + 1 < n_pairs:
                angles(n, p + 1)
            if p == n_pairs - 1:
                angles(n + 2, 3)
            turn_pair(n, p)
    base = 0
    for pairs in ROUND_PAIRS:
        for p in range(len(pairs)):
            for first in (base, STEPS + base):
                rows = pl.ds(first + p * SWEEPS, SWEEPS)
                if p:
                    turn_out[0, rows, :] = pltpu.roll(turn_out[0, rows, :], LANES - p * HALO, 1)
        base += len(pairs) * SWEEPS
    turn_out[0, pl.ds(EIGEN_ROW, 1), :] = tt[0] * (1.0 / ROOT_ROWS)
    turn_out[0, pl.ds(EIGEN_ROW + 1, 1), :] = bb[0] * (1.0 / ROOT_ROWS)
    turn_out[0, pl.ds(EIGEN_ROW + 2, 6), :] = jnp.zeros((6, LANES), jnp.float32)
    for copy in range(1, PARTS):
        turn_out[copy] = turn_out[0]


def widened(turns, wide):
    for part in range(PARTS):
        wide[:, pl.ds(part * LANES, LANES)] = turns[part]


def turned_pair(wide, row, source, target, count, finish):
    for k in range(SWEEPS):
        c = jnp.broadcast_to(wide[pl.ds(row + k, 1), :], (8, WIDTH))
        s = jnp.broadcast_to(wide[pl.ds(STEPS + row + k, 1), :], (8, WIDTH))
        for i in range(count):
            rows = pl.ds(8 * i, 8)
            t, b = source(i) if k == 0 else (target[0][rows, :], target[1][rows, :])
            t, b = c * t + s * b, c * b - s * t
            if k + 1 == SWEEPS:
                finish(i, t, b)
            else:
                target[0][rows, :] = t
                target[1][rows, :] = pltpu.roll(b, WIDTH - 1, 1)


def row_of(pair_round, even_pair, odd_pair):
    base = SWEEPS * sum(len(pairs) for pairs in ROUND_PAIRS[:pair_round])
    return jnp.where(even_slot(), base + SWEEPS * even_pair, base + SWEEPS * odd_pair)


def middle_kernel(back, pair_out, pair_in, turns, eigen_out, near_out, done_out, wide, t0, b0, t1, b1):
    rows_all = back.shape[0]
    count = rows_all // 8
    even = even_slot()
    widened(turns, wide)

    def parts(i):
        rows, low = pl.ds(8 * i, 8), pl.ds(rows_all + 8 * i, 8)
        return rows, low

    def outer(i):
        rows, low = parts(i)
        far = back[rows, :]
        return jnp.where(even, far, pair_out[rows, :]), jnp.where(even, pair_out[low, :], far)

    def inner(i):
        rows, low = parts(i)
        return (
            jnp.where(even, pair_out[rows, :], pair_in[rows, :]),
            jnp.where(even, pair_in[low, :], pair_out[low, :]),
        )

    def keep_outer(i, t, b):
        t0[parts(i)[0], :] = jnp.where(even, t, pltpu.roll(b, WIDTH - 1, 1))

    def keep_inner(i, t, b):
        rows = parts(i)[0]
        t1[rows, :] = t
        b1[rows, :] = pltpu.roll(b, WIDTH - 1, 1)
        near_out[rows, :] = jnp.where(even, t, b1[rows, :])

    def second(i):
        rows = parts(i)[0]
        kept = t0[rows, :]
        return jnp.where(even, kept, t1[rows, :]), jnp.where(even, b1[rows, :], kept)

    def keep_second(i, t, b):
        done_out[parts(i)[0], :] = jnp.where(even, t, pltpu.roll(b, WIDTH - 1, 1))

    turned_pair(wide, row_of(0, 0, 2), outer, (t0, b0), count, keep_outer)
    turned_pair(wide, row_of(0, 1, 1), inner, (t1, b1), count, keep_inner)
    turned_pair(wide, row_of(1, 0, 1), second, (t1, b1), count, keep_second)

    eigen_out[pl.ds(0, WIDTH)] = wide[EIGEN_ROW, :]
    bottom = pltpu.roll(wide[pl.ds(EIGEN_ROW + 1, 1), :], 4 * SWEEPS, 1)
    eigen_out[pl.ds(WIDTH, WIDTH)] = bottom[0]


def last_kernel(pair_in, ahead, near, done, turns, projected_out, wide, t0, b0):
    rows_all = ahead.shape[0]
    count = rows_all // 8
    even = even_slot()
    widened(turns, wide)

    def first(i):
        rows, low = pl.ds(8 * i, 8), pl.ds(rows_all + 8 * i, 8)
        far = ahead[rows, :]
        return jnp.where(even, pair_in[rows, :], far), jnp.where(even, far, pair_in[low, :])

    def keep(i, t, b):
        t0[pl.ds(8 * i, 8), :] = jnp.where(even, pltpu.roll(b, WIDTH - 1, 1), t)

    def with_kept(other):
        def source(i):
            rows = pl.ds(8 * i, 8)
            kept, held = t0[rows, :], other[rows, :]
            return jnp.where(even, held, kept), jnp.where(even, kept, held)

        return source

    def write(i, t, b):
        rows = pl.ds(8 * i, 8)
        b = pltpu.roll(b, 4 * SWEEPS - 1, 1)
        projected_out[rows, pl.ds(0, WIDTH)] = t * t
        projected_out[rows, pl.ds(WIDTH, WIDTH)] = b * b

    turned_pair(wide, row_of(0, 2, 0), first, (t0, b0), count, keep)
    turned_pair(wide, row_of(1, 1, 0), with_kept(near), (t0, b0), count, keep)
    turned_pair(wide, row_of(2, 0, 0), with_kept(done), (t0, b0), count, write)


def call(kernel, outs, scratch, args, flops):
    f32 = jnp.float32
    vmem = pl.BlockSpec(memory_space=pltpu.VMEM)
    shapes = tuple(jax.ShapeDtypeStruct(shape, f32) for shape in outs)
    moved = sum(a.size * a.dtype.itemsize for a in args) + sum(4 * s.size for s in shapes)
    return pl.pallas_call(
        kernel,
        out_shape=shapes,
        in_specs=[vmem] * len(args),
        out_specs=tuple(vmem for _ in shapes),
        scratch_shapes=[pltpu.VMEM(shape, f32) for shape in scratch],
        compiler_params=pltpu.CompilerParams(vmem_limit_bytes=24 * MEGA),
        cost_estimate=pl.CostEstimate(flops=flops, bytes_accessed=moved, transcendentals=0),
    )(*args)


def swapped(shard, by):
    length = lax.axis_size("blk")
    return lax.ppermute(
        shard, "blk", [((i + (by if i % 2 == 0 else -by)) % length, i) for i in range(length)]
    )


def body(root_rows, gradient):
    rows = gradient.shape[0]
    back_root, both_root, ahead_root, turn0 = call(
        first_kernel,
        [(CHUNK_ROWS, LANES), (2 * CHUNK_ROWS, LANES), (CHUNK_ROWS, LANES), (2 * SWEEPS, WIDTH)],
        [(ROOT_ROWS, WIDTH)] * 3 + [(ROOT_ROWS, 2 * LANES)],
        [root_rows],
        16 * ROOT_ROWS * WIDTH * SWEEPS,
    )
    root3 = swapped(ahead_root, 3)
    root0 = swapped(back_root, -3)
    root1 = swapped(both_root, -1)
    root2 = swapped(both_root, 1)
    back_grad, both_grad, ahead_grad = call(
        gradient_first_kernel,
        [(rows, WIDTH), (2 * rows, WIDTH), (rows, WIDTH)],
        [],
        [gradient, turn0],
        8 * rows * WIDTH * SWEEPS,
    )
    def after(value, *others):
        return lax.optimization_barrier((value, *others))[0]

    grad1 = swapped(after(both_grad, root0), -1)
    grad2 = swapped(after(both_grad, root3), 1)
    grad0 = swapped(after(back_grad, root1), -3)
    grad3 = swapped(after(ahead_grad, root1), 3)
    (turns,) = call(
        cone_kernel,
        [(PARTS, ANGLE_ROWS, LANES)],
        [(10, ROOT_ROWS, LANES)],
        [root0, root1, root2, root3],
        16 * CHUNK_ROWS * LANES * STEPS,
    )
    reps = lax.axis_size("rep")
    near = reps // PARTS
    groups = [[x * near + z for x in range(PARTS)] for z in range(near)]
    turns = lax.all_to_all(turns, "rep", 0, 0, axis_index_groups=groups)
    block, angles = (rows, WIDTH), (ANGLE_ROWS, WIDTH)
    eigen, near_block, done_block = call(
        middle_kernel,
        [(2 * WIDTH,), block, block],
        [angles] + [block] * 4,
        [grad0, grad1, grad2, turns],
        4 * rows * WIDTH * STEPS,
    )
    (projected,) = call(
        last_kernel,
        [(rows, 2 * WIDTH)],
        [angles] + [block] * 2,
        [grad2, grad3, near_block, done_block, turns],
        4 * rows * WIDTH * STEPS,
    )
    return eigen, projected


def solution(mesh):
    return jax.shard_map(
        body,
        mesh=mesh,
        in_specs=(P(None, "blk"), P("rep", "blk")),
        out_specs=(P("blk"), P("rep", "blk")),
        check_vma=False,
    )
```
